128 devices in a mesh: gx: 32 (over z, x, core), gy: 4 (over y).
Axes of the slice: x: 4, y: 4, z: 4, core: 2. Of those that a mesh axis runs over, the one named last changes fastest.
Arguments:
- node_feats: bfloat16 [32768, 6272], P(('gx', 'gy')), may hold values from -6 to 6
- halo_index: int32 [128, 4, 32], P(('gx', 'gy')), may hold values from 0 to 255
- edge_source: int32 [16384, 32], P(('gx', 'gy')), may hold values from 0 to 383, as said below
- edge_target: int32 [16384, 32], P(('gx', 'gy')), may hold values from 0 to 2
- edge_length: bfloat16 [16384, 32], P(('gx', 'gy')), may hold values from 0.796875 to 5.5
- edge_harmonics: bfloat16 [16384, 32, 49], P(('gx', 'gy')), may hold values from -4 to 4
- block_peer: int32 [128, 32], P(('gx', 'gy')), may hold values from 0 to 32, as said below
- radial_in: bfloat16 [128, 600], replicated, may hold values from -2 to 2
- radial_out: bfloat16 [600, 896], replicated, may hold values from -0.25 to 0.25
- mix_weight: bfloat16 [7, 128, 128], replicated, may hold values from -0.5 to 0.5
- harmonic_weight: bfloat16 [128, 128], replicated, may hold values from -0.5 to 0.5
- update_weight: bfloat16 [7, 128, 128], replicated, may hold values from -0.25 to 0.25
- norm_gain: float32 [7, 128], replicated, may hold values from 0.1 to 1.9
Outputs:
- updated: bfloat16 [32768, 6272], P(('gx', 'gy'))
The draws below stay inside these ranges and needn't reach their ends.
Inputs may be any that keep to these rules, and one draw needn't show every extreme that they name: `block_peer`: in each row the entries below 32 are distinct. In every gy column some gx index is named by every device of that column. `edge_target`: 2 marks an empty edge slot. `edge_source`: the edges of each block have exactly 16 distinct sources.
All inputs are finite; a program needn't handle non-finite values.
Results may differ from the reference program's by a relative error of at most 0.0053.
Values may be sent and summed in bfloat16 or wider, within the bound.
A program may use at most 128 MiB of HBM per device.

```python
import jax
import jax.numpy as jnp
import numpy as np
from jax import lax

LMAX = 6
DEG = 7
COEF = 49
C = 128
HID = 600
RB = 128
FEAT = 6272
EB = 32
UNIQ = 16
TB = 2
KEEP = 96
HALO = 32
BLOCKS_DEV = 128
NODE_DEV = 256
NODES = 32768
BLOCKS = 16384
N_GX = 32
N_GY = 4
DEVICES = 128


def draw_block_peer(key, part):
    key = jax.random.fold_in(key, 7)
    key_counts, key_scores, key_favoured = jax.random.split(key, 3)
    row_count = DEVICES
    column_count = DEVICES // N_GX
    counts = jax.random.randint(key_counts, (row_count,), 1, N_GX + 1)
    counts = counts.at[0].set(N_GX)
    slot_ids = jnp.arange(N_GX, dtype=jnp.int32)
    scores = jax.random.randint(key_scores, (row_count, N_GX), 0, 1 << 20) * N_GX + slot_ids[None, :]
    favoured = jax.random.randint(key_favoured, (column_count,), 0, N_GX)
    row_favoured = favoured[jnp.arange(row_count, dtype=jnp.int32) % column_count]
    scores = jnp.where(slot_ids[None, :] == row_favoured[:, None], -1, scores)
    ordering = jnp.argsort(scores, axis=1, stable=True).astype(jnp.int32)
    return jnp.where(slot_ids[None, :] < counts[:, None], ordering, N_GX).astype(jnp.int32)


def draw_edge_source(key, part):
    key = jax.random.fold_in(key, 11)
    key_offset, key_slot, key_order = jax.random.split(key, 3)
    table_rows = NODE_DEV + 4 * HALO
    bin_width = table_rows // UNIQ
    bin_ids = jnp.arange(UNIQ, dtype=jnp.int32)
    offsets = jax.random.randint(key_offset, (BLOCKS, UNIQ), 0, bin_width)
    distinct_rows = bin_ids[None, :] * bin_width + offsets
    edge_ids = jnp.arange(EB, dtype=jnp.int32)
    extra_slots = jax.random.randint(key_slot, (BLOCKS, EB), 0, UNIQ)
    slots = jnp.where(edge_ids[None, :] < UNIQ, edge_ids[None, :], extra_slots)
    scores = jax.random.randint(key_order, (BLOCKS, EB), 0, 1 << 20) * EB + edge_ids[None, :]
    ordering = jnp.argsort(scores, axis=1, stable=True).astype(jnp.int32)
    slots = jnp.take_along_axis(slots, ordering, axis=1)
    return jnp.take_along_axis(distinct_rows, slots, axis=1).astype(jnp.int32)


def plant(values, own_key, least, largest):
    longest = values.shape.index(max(values.shape))
    spots = []
    for shift in (0, 1):
        where = [jax.random.randint(jax.random.fold_in(own_key, axis), (), 0, length) for axis, length in enumerate(values.shape)]
        where[longest] = (where[longest] + shift) % values.shape[longest]
        spots.append(tuple(where))
    return values.at[spots[0]].set(least).at[spots[1]].set(largest)


def shard_levels(key, dims, cuts, smallest, top_value):
    level = 1.0
    for position, parts in cuts:
        draws = jax.random.uniform(jax.random.fold_in(jax.random.fold_in(key, 6), position), (parts,), jnp.float32, smallest / len(cuts), top_value / len(cuts))
        level = level * jnp.repeat(jnp.exp(draws), dims[position] // parts).reshape((-1,) + (1,) * (len(dims) - 1 - position))
    return level


def scatter_about(key, shape, deviation, reach, cuts=(), kind=jnp.bfloat16):
    values = jax.random.normal(key, shape, jnp.float32) * deviation
    if len(cuts) > 0:
        values = shard_levels(key, shape, cuts, -0.22, 0.18) * values
    return jnp.clip(values, min=-reach, max=reach).astype(kind)


def setup_inputs(seed: int = 0) -> dict:
    splits = jax.random.split(jax.random.key(seed), 14)
    node_feats = scatter_about(splits[0], (NODES, FEAT), 1.0, 6.0, ((0, 128),))
    halo_index = plant(jax.random.randint(splits[1], (DEVICES, 4, HALO), 0, NODE_DEV), jax.random.fold_in(splits[1], 1), 0, NODE_DEV - 1).astype(jnp.int32)
    edge_source = draw_edge_source(jax.random.fold_in(splits[13], 71), 0)
    edge_target = plant(jax.random.randint(splits[3], (BLOCKS, EB), 0, TB + 1), jax.random.fold_in(splits[3], 1), 0, TB).astype(jnp.int32)
    edge_length = jnp.clip(0.796875 + 4.703125 * jax.random.uniform(splits[4], (BLOCKS, EB), jnp.float32) ** shard_levels(splits[4], (BLOCKS, EB), ((0, 128),), -0.2, 0.2), 0.796875, 5.5).astype(jnp.bfloat16)
    edge_harmonics = scatter_about(splits[5], (BLOCKS, EB, COEF), 1.0, 4.0, ((0, 128),))
    block_peer = draw_block_peer(jax.random.fold_in(splits[13], 71), 0)
    radial_in = scatter_about(splits[7], (RB, HID), 8 ** -0.5, 2.0)
    radial_out = scatter_about(splits[8], (HID, DEG * C), HID ** -0.5, 0.25)
    mix_weight = scatter_about(splits[9], (DEG, C, C), C ** -0.5, 0.5)
    harmonic_weight = scatter_about(splits[10], (C, C), C ** -0.5, 0.5)
    update_weight = scatter_about(splits[11], (DEG, C, C), (4 * C) ** -0.5, 0.25)
    norm_gain = jnp.clip(1.0 + 0.18 * jax.random.normal(splits[12], (DEG, C), jnp.float32), 0.1, 1.9)
    return {"node_feats": node_feats, "halo_index": halo_index, "edge_source": edge_source, "edge_target": edge_target, "edge_length": edge_length, "edge_harmonics": edge_harmonics, "block_peer": block_peer, "radial_in": radial_in, "radial_out": radial_out, "mix_weight": mix_weight, "harmonic_weight": harmonic_weight, "update_weight": update_weight, "norm_gain": norm_gain}


cutoff_radius = 6.0
group_size = 8
norm_eps = 1e-06

def degree_index():
    return np.repeat(np.arange(LMAX + 1), 2 * np.arange(LMAX + 1) + 1)

def radial_features(distance):
    centers = cutoff_radius * (jnp.arange(RB, dtype=jnp.float32) + 0.5) / RB
    spread = 2.0 * cutoff_radius / RB
    envelope = 0.5 * (jnp.cos(jnp.pi * distance / cutoff_radius) + 1.0)
    offsets = (distance[:, None] - centers[None, :]) / spread
    return (jnp.exp(-0.5 * offsets * offsets) * envelope[:, None]).astype(jnp.bfloat16)

def edge_messages(sources_feat, distance, harmonics, radial_in, radial_out, mix_weight, harmonic_weight):
    basis_vals = radial_features(distance.astype(jnp.float32))
    hidden = jax.nn.silu(jnp.dot(basis_vals, radial_in, preferred_element_type=jnp.float32)).astype(jnp.bfloat16)
    gate_vals = jnp.dot(hidden, radial_out, preferred_element_type=jnp.float32).astype(jnp.bfloat16)
    gate_vals = gate_vals.reshape(-1, LMAX + 1, C)
    pieces = []
    for degree in range(LMAX + 1):
        first_row = degree * degree
        last_row = (degree + 1) * (degree + 1)
        scaled = (sources_feat[:, first_row:last_row, :].astype(jnp.float32) * gate_vals[:, degree:degree + 1, :].astype(jnp.float32)).astype(jnp.bfloat16)
        pieces.append(jnp.einsum('erc,cd->erd', scaled.astype(jnp.float32), mix_weight[degree].astype(jnp.float32)))
    mixed_rows = jnp.concatenate(pieces, axis=1)
    scalar = jnp.dot(sources_feat[:, 0, :], harmonic_weight, preferred_element_type=jnp.float32)
    return (mixed_rows + harmonics.astype(jnp.float32)[:, :, None] * scalar[:, None, :]).astype(jnp.bfloat16)

def block_sums(messages, targets):
    onehot = (targets[:, None, :] == jnp.arange(TB, dtype=jnp.int32)[None, :, None]).astype(jnp.float32)
    return jnp.einsum('gte,gef->gtf', onehot, messages.astype(jnp.float32)).astype(jnp.bfloat16)

def node_update(node_rows, gathered, update_weight, norm_gain):
    pieces = []
    for degree in range(LMAX + 1):
        first_row = degree * degree
        last_row = (degree + 1) * (degree + 1)
        pieces.append(jnp.einsum('nrc,cd->nrd', gathered[:, first_row:last_row, :].astype(jnp.float32), update_weight[degree].astype(jnp.float32)))
    combined = node_rows.astype(jnp.float32).reshape(-1, COEF, C) + jnp.concatenate(pieces, axis=1)
    inverse_rms = lax.rsqrt(lax.optimization_barrier(jnp.mean(combined * combined, axis=(1, 2), keepdims=True)) + norm_eps)
    gain_rows = norm_gain[degree_index()]
    return (combined * inverse_rms * gain_rows[None]).astype(jnp.bfloat16).reshape(-1, FEAT)

def reference(node_feats, halo_index, edge_source, edge_target, edge_length, edge_harmonics, block_peer, radial_in, radial_out, mix_weight, harmonic_weight, update_weight, norm_gain):
    node_blocks = node_feats.reshape(DEVICES, NODE_DEV, FEAT)
    group_count = BLOCKS_DEV // group_size
    source_rows = edge_source.reshape(DEVICES, group_count, group_size, EB)
    target_rows = edge_target.reshape(DEVICES, group_count, group_size, EB)
    length_rows = edge_length.reshape(DEVICES, group_count, group_size, EB)
    harmonic_rows = edge_harmonics.reshape(DEVICES, group_count, group_size, EB, COEF)

    def per_device(device):
        cycle_pos = device // N_GY
        column_pos = device % N_GY
        neighbours = [(cycle_pos - 1) % N_GX * N_GY + column_pos, (cycle_pos + 1) % N_GX * N_GY + column_pos, cycle_pos * N_GY + (column_pos - 1) % N_GY, cycle_pos * N_GY + (column_pos + 1) % N_GY]
        pieces = [node_blocks[device]]
        for direction in range(4):
            sender = neighbours[direction]
            pieces.append(node_blocks[sender][halo_index[sender, direction]])
        source_table = jnp.concatenate(pieces, axis=0)

        def per_group(inputs):
            sources, targets, distance, harmonics = inputs
            gathered = source_table[sources.reshape(-1)].reshape(-1, COEF, C)
            message = edge_messages(gathered, distance.reshape(-1), harmonics.reshape(-1, COEF), radial_in, radial_out, mix_weight, harmonic_weight)
            return block_sums(message.reshape(group_size, EB, FEAT), targets)
        block_totals = lax.map(per_group, (source_rows[device], target_rows[device], length_rows[device], harmonic_rows[device])).reshape(BLOCKS_DEV, TB, FEAT)
        present_flags = jnp.concatenate([jnp.ones((KEEP,), dtype=bool), block_peer[device] < N_GX])
        block_totals = jnp.where(present_flags[:, None, None], block_totals, jnp.zeros_like(block_totals))
        return node_update(node_blocks[device], block_totals.reshape(NODE_DEV, COEF, C), update_weight, norm_gain)
    result = lax.map(per_device, jnp.arange(DEVICES, dtype=jnp.int32))
    return result.reshape(NODES, FEAT)
```

```python
import functools

import jax
import jax.numpy as jnp
import numpy as np
from jax import lax
from jax.experimental import pallas as pl
from jax.experimental.pallas import tpu as pltpu
from jax.sharding import PartitionSpec as P

LMAX = 6
DEG = 7
COEF = 49
C = 128
HID = 600
RB = 128
FEAT = 6272
EB = 32
TB = 2
KEEP = 96
BLOCKS = 128
NODES = 256
HALO = 32
TABLE = NODES + 4 * HALO
GROUP = 8
GROUPS = BLOCKS // GROUP
GE = GROUP * EB
GN = GROUP * TB
LENGTHS = 384
ROWS = 48
CHUNK = 4
CHUNKS = EB // CHUNK + 1
SLOTS = CHUNK * CHUNKS
ZERO_ROW = TABLE

cutoff_radius = 6.0
norm_eps = 1e-06

F32 = jnp.float32
BF16 = jnp.bfloat16
I32 = jnp.int32

DEGREE_OF = np.repeat(np.arange(LMAX + 1), 2 * np.arange(LMAX + 1) + 1)
TILES = ((1, 6), (2, 5), (3, 4))
PLACE = {}
for _tile, _pair in enumerate(TILES):
    _at = 16 * _tile
    for _degree in _pair:
        for _lm in range(_degree * _degree, (_degree + 1) * (_degree + 1)):
            PLACE[_lm] = _at
            _at += 1


def length_index(length):
    r = length.astype(F32)
    f = jnp.where(
        r < 1.0,
        (r - 0.796875) * 256.0,
        jnp.where(
            r < 2.0,
            (r - 1.0) * 128.0 + 52.0,
            jnp.where(r < 4.0, (r - 2.0) * 64.0 + 180.0, (r - 4.0) * 32.0 + 308.0),
        ),
    )
    return f.astype(I32)


def length_of(i):
    return jnp.where(
        i < 52.0,
        0.796875 + i / 256.0,
        jnp.where(
            i < 180.0,
            1.0 + (i - 52.0) / 128.0,
            jnp.where(i < 308.0, 2.0 + (i - 180.0) / 64.0, 4.0 + (i - 308.0) / 32.0),
        ),
    )


def outgoing_kernel(index_ref, nodes_ref, out_ref):
    row = lax.broadcasted_iota(I32, (4 * HALO, NODES), 1)
    onehot = (row == index_ref[...]).astype(F32).astype(BF16)
    for at in range(0, FEAT, 896):
        out_ref[:, at : at + 896] = jnp.dot(
            onehot, nodes_ref[:, at : at + 896], preferred_element_type=F32
        ).astype(BF16)


def fill_gates(radial_in_ref, radial_out_ref, gate_ref, gate0_ref, table_ref):
    i = lax.broadcasted_iota(I32, (LENGTHS, RB), 0).astype(F32)
    r = length_of(i)
    k = lax.broadcasted_iota(I32, (LENGTHS, RB), 1).astype(F32)
    centers = cutoff_radius * (k + 0.5) / RB
    spread = 2.0 * cutoff_radius / RB
    envelope = 0.5 * (jnp.cos(jnp.pi * r / cutoff_radius) + 1.0)
    offsets = (r - centers) / spread
    basis = (jnp.exp(-0.5 * offsets * offsets) * envelope).astype(BF16)
    hidden = jax.nn.silu(jnp.dot(basis, radial_in_ref[...], preferred_element_type=F32)).astype(BF16)
    gate = jnp.dot(hidden, radial_out_ref[...], preferred_element_type=F32).astype(BF16)
    gate0_ref[...] = gate[:, :C]
    gate_ref[...] = gate.astype(F32)
    row = lax.broadcasted_iota(I32, (16, C), 0)

    @pl.loop(0, LENGTHS // 8)
    def _(g):
        rows = [gate_ref[pl.ds(g * 8, 8), d * C : (d + 1) * C] for d in range(DEG)]
        for j in range(8):
            for tile, (low, high) in enumerate(TILES):
                first = jnp.broadcast_to(rows[low][j : j + 1], (16, C))
                second = jnp.broadcast_to(rows[high][j : j + 1], (16, C))
                table_ref[g * 8 + j, 16 * tile : 16 * tile + 16, :] = jnp.where(
                    row < 2 * low + 1, first, second
                ).astype(BF16)


def spread_rows(source_ref, count, base, wide_ref, table_ref):
    @pl.loop(0, count // 16)
    def _(g):
        at = pl.multiple_of(g * 16, 16)
        for lm in range(1, COEF):
            wide_ref[pl.ds(PLACE[lm], 16, stride=ROWS), :] = source_ref[
                pl.ds(at, 16), lm * C : (lm + 1) * C
            ].astype(F32)
        for j in range(16):
            table_ref[base + at + j] = wide_ref[j * ROWS : (j + 1) * ROWS, :].astype(BF16)


def fill_slots(payload_ref, target_ref, slot_ref):
    payload = payload_ref[...]
    target = target_ref[...]
    lower = (
        lax.broadcasted_iota(I32, (EB, EB), 0) > lax.broadcasted_iota(I32, (EB, EB), 1)
    ).astype(F32)
    zero = (target == 0).astype(F32)
    one = (target == 1).astype(F32)
    rank0 = jnp.dot(lower, zero, preferred_element_type=F32).astype(I32)
    rank1 = jnp.dot(lower, one, preferred_element_type=F32).astype(I32)
    slot = jnp.where(target == 0, rank0, jnp.where(target == 1, SLOTS - 1 - rank1, -1))
    nothing = ZERO_ROW * 512
    relative = payload - nothing
    for s in range(SLOTS):
        slot_ref[s : s + 1, :] = (
            jnp.sum(jnp.where(slot == s, relative, 0), axis=0, keepdims=True) + nothing
        )
    count0 = jnp.sum(zero, axis=0, keepdims=True).astype(I32)
    slot_ref[SLOTS : SLOTS + 1, :] = (count0 + (CHUNK - 1)) // CHUNK


def sum_edges(slots, table_ref, gates_ref, sums_ref):
    @pl.loop(0, BLOCKS)
    def _(b):
        first = slots[SLOTS, b]
        total0 = jnp.zeros((ROWS, C), F32)
        total1 = jnp.zeros((ROWS, C), F32)
        for j in range(CHUNKS):
            parts = []
            for k in range(CHUNK):
                p = slots[j * CHUNK + k, b]
                parts.append(
                    table_ref[lax.shift_right_logical(p, 9)] * gates_ref[lax.bitwise_and(p, 511)]
                )
            part = ((parts[0] + parts[1]) + (parts[2] + parts[3])).astype(F32)
            mine = j < first
            total0 = total0 + jnp.where(mine, part, 0.0)
            total1 = total1 + jnp.where(mine, 0.0, part)
        at = pl.multiple_of(b * (2 * ROWS), 8)
        sums_ref[pl.ds(at, ROWS), :] = total0
        sums_ref[pl.ds(at + ROWS, ROWS), :] = total1


def harmonic_sums(
    source_col_ref, length_col_ref, target_row_ref, harm_ref, scalars_ref, gate0_ref, harm_sums_ref, first_ref
):
    node = lax.broadcasted_iota(I32, (GN, GE), 0)
    edge = lax.broadcasted_iota(I32, (GN, GE), 1)
    same_block = lax.shift_right_logical(node, 1) == lax.shift_right_logical(edge, 5)
    wanted = jnp.where(same_block, lax.bitwise_and(node, 1), -1)
    row = lax.broadcasted_iota(I32, (GE, TABLE), 1)
    for g in range(GROUPS):
        pick = (source_col_ref[:, g : g + 1] == row).astype(F32).astype(BF16)
        scalars = jnp.dot(pick, scalars_ref[...], preferred_element_type=F32).astype(BF16)
        pick = (length_col_ref[:, g : g + 1] == row).astype(F32).astype(BF16)
        gates = jnp.dot(pick, gate0_ref[...], preferred_element_type=F32).astype(BF16)
        mask = (target_row_ref[g : g + 1, :] == wanted).astype(F32)
        first_ref[g * GN : (g + 1) * GN, :] = jnp.dot(
            mask.astype(BF16), scalars * gates, preferred_element_type=F32
        ).astype(BF16)
        harm = harm_ref[g].astype(F32)
        left = jnp.concatenate([(harm[lm : lm + 1, :] * mask).astype(BF16) for lm in range(COEF)], axis=0)
        right = jnp.dot(left, scalars, preferred_element_type=F32).astype(BF16)
        for lm in range(COEF):
            harm_sums_ref[lm, g * GN : (g + 1) * GN, :] = right[lm * GN : (lm + 1) * GN]


def update_nodes(
    nodes_ref, sums_ref, first_ref, harm_sums_ref, mix_ref, harmonic_ref, update_ref, gain_ref, combined_ref, out_ref
):
    squares = jnp.zeros((NODES, C), F32)
    for degree in range(DEG):
        update = update_ref[degree]
        both = jnp.concatenate([mix_ref[degree], harmonic_ref[...]], axis=0)
        weight = jnp.dot(both, update, preferred_element_type=F32).astype(BF16)
        for lm in range(degree * degree, (degree + 1) * (degree + 1)):
            if lm == 0:
                left = first_ref[...]
            else:
                left = sums_ref[pl.ds(PLACE[lm], NODES, stride=ROWS), :].astype(BF16)
            left = jnp.concatenate([left, harm_sums_ref[lm]], axis=1)
            mixed = jnp.dot(left, weight, preferred_element_type=F32)
            value = nodes_ref[:, lm * C : (lm + 1) * C].astype(F32) + mixed
            combined_ref[:, lm * C : (lm + 1) * C] = value
            squares = squares + value * value
    mean = jnp.sum(squares, axis=1, keepdims=True) / FEAT
    inverse = lax.rsqrt(mean + norm_eps)
    for lm in range(COEF):
        degree = int(DEGREE_OF[lm])
        out_ref[:, lm * C : (lm + 1) * C] = (
            combined_ref[:, lm * C : (lm + 1) * C] * inverse * gain_ref[degree : degree + 1, :]
        ).astype(BF16)


def layer_kernel(
    nodes_ref,
    halo0_ref,
    halo1_ref,
    halo2_ref,
    halo3_ref,
    payload_ref,
    target_ref,
    source_col_ref,
    length_col_ref,
    target_row_ref,
    harm_ref,
    radial_in_ref,
    radial_out_ref,
    mix_ref,
    harmonic_ref,
    update_ref,
    gain_ref,
    out_ref,
    gate_ref,
    gate0_ref,
    gates_ref,
    wide_ref,
    table_ref,
    scalars_ref,
    slot_ref,
    slots,
    sums_ref,
    first_ref,
    harm_sums_ref,
    combined_ref,
    slot_sem,
):
    fill_slots(payload_ref, target_ref, slot_ref)
    copy = pltpu.make_async_copy(slot_ref, slots, slot_sem)
    copy.start()
    fill_gates(radial_in_ref, radial_out_ref, gate_ref, gate0_ref, gates_ref)
    spread_rows(nodes_ref, NODES, 0, wide_ref, table_ref)
    scalars_ref[:NODES, :] = nodes_ref[:, :C]
    for k, halo_ref in enumerate((halo0_ref, halo1_ref, halo2_ref, halo3_ref)):
        base = NODES + HALO * k
        spread_rows(halo_ref, HALO, base, wide_ref, table_ref)
        scalars_ref[base : base + HALO, :] = halo_ref[:, :C]
    table_ref[ZERO_ROW] = jnp.zeros((ROWS, C), BF16)
    copy.wait()
    sum_edges(slots, table_ref, gates_ref, sums_ref)
    harmonic_sums(
        source_col_ref,
        length_col_ref,
        target_row_ref,
        harm_ref,
        scalars_ref,
        gate0_ref,
        harm_sums_ref,
        first_ref,
    )
    update_nodes(
        nodes_ref,
        sums_ref,
        first_ref,
        harm_sums_ref,
        mix_ref,
        harmonic_ref,
        update_ref,
        gain_ref,
        combined_ref,
        out_ref,
    )


def layer(*arrays):
    return pl.pallas_call(
        layer_kernel,
        out_shape=jax.ShapeDtypeStruct((NODES, FEAT), BF16),
        in_specs=[pl.BlockSpec(memory_space=pltpu.VMEM)] * len(arrays),
        out_specs=pl.BlockSpec(memory_space=pltpu.VMEM),
        scratch_shapes=[
            pltpu.VMEM((LENGTHS, DEG * C), F32),
            pltpu.VMEM((LENGTHS, C), BF16),
            pltpu.VMEM((LENGTHS, ROWS, C), BF16),
            pltpu.VMEM((16 * ROWS, C), F32),
            pltpu.VMEM((TABLE + 1, ROWS, C), BF16),
            pltpu.VMEM((TABLE, C), BF16),
            pltpu.VMEM((40, BLOCKS), I32),
            pltpu.SMEM((40, BLOCKS), I32),
            pltpu.VMEM((NODES * ROWS, C), F32),
            pltpu.VMEM((NODES, C), BF16),
            pltpu.VMEM((COEF, NODES, C), BF16),
            pltpu.VMEM((NODES, FEAT), F32),
            pltpu.SemaphoreType.DMA,
        ],
        compiler_params=pltpu.CompilerParams(vmem_limit_bytes=60 * 1024 * 1024),
        name="layer",
    )(*arrays)


def outgoing_rows(halo_index, node_feats):
    return pl.pallas_call(
        outgoing_kernel,
        out_shape=jax.ShapeDtypeStruct((4 * HALO, FEAT), BF16),
        in_specs=[pl.BlockSpec(memory_space=pltpu.VMEM)] * 2,
        out_specs=pl.BlockSpec(memory_space=pltpu.VMEM),
        compiler_params=pltpu.CompilerParams(vmem_limit_bytes=32 * 1024 * 1024),
        name="outgoing",
    )(halo_index.reshape(4 * HALO, 1), node_feats)


def edge_lists(edge_source, edge_target, edge_length, edge_harmonics, block_peer, peers):
    live = jnp.concatenate([jnp.ones((KEEP,), bool), block_peer[0] < peers])
    target = jnp.where(live[:, None], edge_target, TB)
    length = length_index(edge_length)
    payload = edge_source * 512 + length
    harm = edge_harmonics.reshape(GROUPS, GE, COEF).transpose(0, 2, 1)
    return (
        payload.T,
        target.T,
        edge_source.reshape(GROUPS, GE).T,
        length.reshape(GROUPS, GE).T,
        target.reshape(GROUPS, GE),
        harm,
    )


def shifted(rows, axis, step):
    size = lax.axis_size(axis)
    return lax.ppermute(rows, axis, [((i - step) % size, i) for i in range(size)])


def per_device(
    node_feats,
    halo_index,
    edge_source,
    edge_target,
    edge_length,
    edge_harmonics,
    block_peer,
    radial_in,
    radial_out,
    mix_weight,
    harmonic_weight,
    update_weight,
    norm_gain,
):
    outgoing = outgoing_rows(halo_index, node_feats)
    arrived = [
        shifted(outgoing[HALO * k : HALO * (k + 1)], axis, step)
        for k, (axis, step) in enumerate((("gx", 1), ("gx", -1), ("gy", 1), ("gy", -1)))
    ]
    lists = edge_lists(
        edge_source, edge_target, edge_length, edge_harmonics, block_peer, lax.axis_size("gx")
    )
    return layer(
        node_feats,
        *arrived,
        *lists,
        radial_in,
        radial_out,
        mix_weight,
        harmonic_weight,
        update_weight,
        norm_gain,
    )


def solution(mesh):
    split = ("gx", "gy")
    in_specs = (
        P(split, None),
        P(split, None, None),
        P(split, None),
        P(split, None),
        P(split, None),
        P(split, None, None),
        P(split, None),
        P(),
        P(),
        P(),
        P(),
        P(),
        P(),
    )
    return jax.shard_map(
        per_device, mesh=mesh, in_specs=in_specs, out_specs=P(split, None), check_vma=False
    )
```

```python
import functools

import jax
import jax.numpy as jnp
import numpy as np
from jax import lax
from jax.experimental import pallas as pl
from jax.experimental.pallas import tpu as pltpu
from jax.sharding import PartitionSpec as P

LMAX = 6
DEG = 7
COEF = 49
C = 128
HID = 600
RB = 128
FEAT = 6272
EB = 32
TB = 2
KEEP = 96
BLOCKS = 128
NODES = 256
HALO = 32
TABLE = NODES + 4 * HALO
GROUP = 8
GROUPS = BLOCKS // GROUP
GE = GROUP * EB
GN = GROUP * TB
LENGTHS = 384
ROWS = 48
CHUNK = 4
CHUNKS = EB // CHUNK + 1
SLOTS = CHUNK * CHUNKS
ZERO_ROW = TABLE

cutoff_radius = 6.0
norm_eps = 1e-06

F32 = jnp.float32
BF16 = jnp.bfloat16
I32 = jnp.int32

DEGREE_OF = np.repeat(np.arange(LMAX + 1), 2 * np.arange(LMAX + 1) + 1)
PARTS = 3
WIDE = 2 * C
HALF = 64
PIECE = 7 * C
PIECES = FEAT // PIECE
MESH = pl.DeviceIdType.MESH


def length_index(length):
    r = length.astype(F32)
    f = jnp.where(
        r < 1.0,
        (r - 0.796875) * 256.0,
        jnp.where(
            r < 2.0,
            (r - 1.0) * 128.0 + 52.0,
            jnp.where(r < 4.0, (r - 2.0) * 64.0 + 180.0, (r - 4.0) * 32.0 + 308.0),
        ),
    )
    return f.astype(I32)


def length_of(i):
    return jnp.where(
        i < 52.0,
        0.796875 + i / 256.0,
        jnp.where(
            i < 180.0,
            1.0 + (i - 52.0) / 128.0,
            jnp.where(i < 308.0, 2.0 + (i - 180.0) / 64.0, 4.0 + (i - 308.0) / 32.0),
        ),
    )


def fill_gates(radial_in_ref, radial_out_ref, gate_ref, gate0_ref, table_ref):
    i = lax.broadcasted_iota(I32, (LENGTHS, RB), 0).astype(F32)
    r = length_of(i)
    k = lax.broadcasted_iota(I32, (LENGTHS, RB), 1).astype(F32)
    centers = cutoff_radius * (k + 0.5) / RB
    spread = 2.0 * cutoff_radius / RB
    envelope = 0.5 * (jnp.cos(jnp.pi * r / cutoff_radius) + 1.0)
    offsets = (r - centers) / spread
    basis = (jnp.exp(-0.5 * offsets * offsets) * envelope).astype(BF16)
    hidden = lax.dot_general(
        basis, radial_in_ref[...], (((1,), (1,)), ((), ())), preferred_element_type=F32
    )
    hidden = jax.nn.silu(hidden).astype(BF16)
    gate = jnp.dot(hidden, radial_out_ref[...], preferred_element_type=F32).astype(BF16)
    gate0_ref[...] = gate[:, :C]
    gate_ref[...] = gate.astype(F32)
    row = lax.broadcasted_iota(I32, (8, C), 0)

    @pl.loop(0, LENGTHS // 8)
    def _(g):
        rows = [gate_ref[pl.ds(g * 8, 8), d * C : (d + 1) * C] for d in range(DEG)]
        at = g * (8 * PARTS)
        for j in range(8):
            tiles = []
            for tile in range(6):
                first = int(DEGREE_OF[1 + 8 * tile])
                last = int(DEGREE_OF[8 + 8 * tile])
                value = jnp.broadcast_to(rows[first][j : j + 1], (8, C))
                if last != first:
                    split = last * last - (1 + 8 * tile)
                    value = jnp.where(
                        row < split, value, jnp.broadcast_to(rows[last][j : j + 1], (8, C))
                    )
                tiles.append(value)
            for i in range(3):
                table_ref[at + j * PARTS + i] = jnp.concatenate(
                    tiles[2 * i : 2 * i + 2], axis=1
                ).astype(BF16)


def spread_rows(source_ref, count, base, wide_ref, table_ref):
    @pl.loop(0, count // 16)
    def _(g):
        at = pl.multiple_of(g * 16, 16)
        for lm in range(1, COEF, 2):
            pair = source_ref[pl.ds(at, 16), lm * C : (lm + 2) * C].astype(F32)
            wide_ref[pl.ds(lm - 1, 16, stride=ROWS), :] = pair[:, :C]
            wide_ref[pl.ds(lm, 16, stride=ROWS), :] = pair[:, C:]
        to = (base + at) * PARTS
        for j in range(16):
            for i in range(3):
                low = j * ROWS + 16 * i
                table_ref[to + j * PARTS + i] = jnp.concatenate(
                    [wide_ref[low : low + 8, :], wide_ref[low + 8 : low + 16, :]], axis=1
                ).astype(BF16)


def column_of(row, size):
    diagonal = lax.broadcasted_iota(I32, (size, size), 0) == lax.broadcasted_iota(I32, (size, size), 1)
    return jnp.sum(jnp.where(diagonal, jnp.broadcast_to(row, (size, size)), 0), axis=1, keepdims=True)


def fill_lists(peer_ref, source_ref, target_ref, length_ref, peers, across_refs, slot_ref):
    peer = jnp.concatenate([jnp.zeros((1, KEEP), I32), peer_ref[...]], axis=1)
    target = jnp.where(peer < peers, target_ref[...], TB)
    source = source_ref[...]
    length = length_index(length_ref[...])
    for ref, value in zip(across_refs, (source, length, target)):
        ref[...] = value.T
    lower = (
        lax.broadcasted_iota(I32, (EB, EB), 0) > lax.broadcasted_iota(I32, (EB, EB), 1)
    ).astype(F32)
    zero = (target == 0).astype(F32)
    one = (target == 1).astype(F32)
    rank0 = jnp.dot(lower, zero, preferred_element_type=F32).astype(I32)
    rank1 = jnp.dot(lower, one, preferred_element_type=F32).astype(I32)
    slot = jnp.where(target == 0, rank0, jnp.where(target == 1, SLOTS - 1 - rank1, -1))
    relative = (source - ZERO_ROW) * PARTS
    length = length * PARTS
    count0 = jnp.sum(zero, axis=0, keepdims=True).astype(I32)
    rows = []
    for s in range(SLOTS):
        rows.append(jnp.sum(jnp.where(slot == s, relative, 0), axis=0, keepdims=True) + ZERO_ROW * PARTS)
    rows.append(lax.shift_right_logical(count0 + (CHUNK - 1), 2))
    rows.append(jnp.zeros((HALF - SLOTS - 1, BLOCKS), I32))
    for s in range(SLOTS):
        rows.append(jnp.sum(jnp.where(slot == s, length, 0), axis=0, keepdims=True))
    rows.append(jnp.zeros((HALF - SLOTS, BLOCKS), I32))
    slot_ref[...] = jnp.concatenate(rows, axis=0).T


def by_group(ref):
    return jnp.concatenate([ref[pl.ds(b, GROUPS, stride=GROUP), :] for b in range(GROUP)], axis=1)


def transposed(x):
    rows = x.shape[1]
    identity = (
        lax.broadcasted_iota(I32, (rows, rows), 0) == lax.broadcasted_iota(I32, (rows, rows), 1)
    ).astype(F32).astype(BF16)
    return lax.dot_general(identity, x, (((1,), (1,)), ((), ())), preferred_element_type=F32)


def harmonic_sums(
    across_refs, harm_ref, scalars_ref, gate0_ref, rows_ref, turned_ref, harm_rows_ref, harm_sums_ref, first_ref
):
    for n, ref in enumerate(across_refs):
        rows_ref[n] = by_group(ref)

    @pl.loop(0, COEF // 7)
    def _(step):
        for n in range(7):
            turned_ref[n] = harm_ref[step * 7 + n].astype(F32).T
            at = pl.multiple_of((step * 7 + n) * GROUPS, GROUPS)
            harm_rows_ref[pl.ds(at, GROUPS), :] = by_group(turned_ref.at[n])

    node = lax.broadcasted_iota(I32, (GN, GE), 0)
    edge = lax.broadcasted_iota(I32, (GN, GE), 1)
    same_block = lax.shift_right_logical(node, 1) == lax.shift_right_logical(edge, 5)
    wanted = jnp.where(same_block, lax.bitwise_and(node, 1), -1)
    across = (((1,), (1,)), ((), ()))
    scalars = transposed(scalars_ref[...]).astype(BF16)
    gate0 = transposed(gate0_ref[...]).astype(BF16)

    @pl.loop(0, GROUPS)
    def _(g):
        row = lax.broadcasted_iota(I32, (TABLE, GE), 0)
        pick = (rows_ref[0, pl.ds(g, 1), :] == row).astype(F32).astype(BF16)
        scalar = jnp.dot(scalars, pick, preferred_element_type=F32).astype(BF16)
        pick = (rows_ref[1, pl.ds(g, 1), :] == row).astype(F32).astype(BF16)
        gate = jnp.dot(gate0, pick, preferred_element_type=F32).astype(BF16)
        mask = (rows_ref[2, pl.ds(g, 1), :] == wanted).astype(F32)
        at = pl.multiple_of(g * GN, GN)
        first_ref[pl.ds(at, GN), :] = lax.dot_general(
            mask.astype(BF16), scalar * gate, across, preferred_element_type=F32
        )
        left = jnp.concatenate(
            [
                (harm_rows_ref[pl.ds(lm * GROUPS + g, 1), :] * mask).astype(BF16)
                for lm in range(COEF)
            ],
            axis=0,
        )
        right = lax.dot_general(left, scalar, across, preferred_element_type=F32)
        for lm in range(COEF):
            harm_sums_ref[lm, pl.ds(at, GN), :] = right[lm * GN : (lm + 1) * GN]


def gather_kernel(
    nodes_hbm,
    halo_hbm,
    peer_hbm,
    source_hbm,
    target_hbm,
    length_hbm,
    radial_in_hbm,
    radial_out_hbm,
    harm_hbm,
    table_ref,
    gates_ref,
    harm_sums_ref,
    first_ref,
    slot_ref,
    halo_ref,
    peer_ref,
    source_ref,
    target_ref,
    length_ref,
    radial_in_ref,
    harm_ref,
    nodes_ref,
    radial_out_ref,
    send_ref,
    arrived_ref,
    gate_ref,
    gate0_ref,
    wide_ref,
    scalars_ref,
    source_across_ref,
    length_across_ref,
    target_across_ref,
    rows_ref,
    turned_ref,
    harm_rows_ref,
    load_sem,
    other_sem,
    send_sem,
    recv_sem,
    peers,
    columns,
):
    p, q = lax.axis_index("gx"), lax.axis_index("gy")
    ahead, behind = lax.rem(p + 1, peers), lax.rem(p + peers - 1, peers)
    above, below = lax.rem(q + 1, columns), lax.rem(q + columns - 1, columns)
    neighbours = ((ahead, q), (behind, q), (p, above), (p, below))

    smalls = []
    for n, (source, target) in enumerate(
        (
            (halo_hbm, halo_ref),
            (peer_hbm, peer_ref),
            (source_hbm, source_ref),
            (target_hbm, target_ref),
            (length_hbm, length_ref),
            (radial_in_hbm, radial_in_ref),
            (radial_out_hbm, radial_out_ref),
            (harm_hbm, harm_ref),
        )
    ):
        smalls.append(pltpu.make_async_copy(source, target, other_sem.at[n]))
    smalls[0].start()
    loads = []
    for c in range(PIECES):
        cut = pl.ds(c * PIECE, PIECE)
        load = pltpu.make_async_copy(nodes_hbm.at[:, cut], nodes_ref.at[:, cut], load_sem.at[c])
        load.start()
        loads.append(load)
    for load in smalls[1:]:
        load.start()

    barrier = pltpu.get_barrier_semaphore()
    for neighbour in neighbours:
        pl.semaphore_signal(barrier, inc=1, device_id=neighbour, device_id_type=MESH)

    smalls[0].wait()
    index = column_of(jnp.concatenate([halo_ref[k : k + 1, :] for k in range(4)], axis=1), 4 * HALO)
    pick = (lax.broadcasted_iota(I32, (4 * HALO, NODES), 1) == index).astype(F32).astype(BF16)
    pl.semaphore_wait(barrier, 4)
    copies = []
    for c in range(PIECES):
        loads[c].wait()
        cut = pl.ds(c * PIECE, PIECE)
        send_ref[:, cut] = jnp.dot(pick, nodes_ref[:, cut], preferred_element_type=F32).astype(BF16)
        for k in (2, 3, 0, 1):
            part = pl.ds(k * HALO, HALO)
            copy = pltpu.make_async_remote_copy(
                src_ref=send_ref.at[part, cut],
                dst_ref=arrived_ref.at[part, cut],
                send_sem=send_sem.at[k, c],
                recv_sem=recv_sem.at[k, c],
                device_id=neighbours[k],
                device_id_type=MESH,
            )
            copy.start()
            copies.append(copy)

    for load in smalls[1:5]:
        load.wait()
    across_refs = (source_across_ref, length_across_ref, target_across_ref)
    fill_lists(peer_ref, source_ref, target_ref, length_ref, peers, across_refs, slot_ref)
    smalls[5].wait()
    smalls[6].wait()
    fill_gates(radial_in_ref, radial_out_ref, gate_ref, gate0_ref, gates_ref)
    spread_rows(nodes_ref, NODES, 0, wide_ref, table_ref)
    table_ref[ZERO_ROW * PARTS :] = jnp.zeros((PARTS, 8, WIDE), BF16)
    smalls[7].wait()
    for copy in copies[:4]:
        copy.wait_recv()
    scalars_ref[:NODES, :] = nodes_ref[:, :C]
    scalars_ref[NODES:, :] = arrived_ref[:, :C]
    harmonic_sums(
        across_refs,
        harm_ref,
        scalars_ref,
        gate0_ref,
        rows_ref,
        turned_ref,
        harm_rows_ref,
        harm_sums_ref,
        first_ref,
    )
    for copy in copies[4:]:
        copy.wait_recv()
    spread_rows(arrived_ref, 4 * HALO, NODES, wide_ref, table_ref)
    for copy in copies:
        copy.wait_send()


def sum_edges(slots, table_ref, gates_ref, sums_ref):
    @pl.loop(0, BLOCKS)
    def _(b):
        first = slots[b, SLOTS]
        total0 = jnp.zeros((PARTS, 8, WIDE), F32)
        total1 = jnp.zeros((PARTS, 8, WIDE), F32)
        for j in range(CHUNKS):
            parts = []
            for k in range(CHUNK):
                at = j * CHUNK + k
                parts.append(
                    table_ref[pl.ds(slots[b, at], PARTS)] * gates_ref[pl.ds(slots[b, HALF + at], PARTS)]
                )
            part = ((parts[0] + parts[1]) + (parts[2] + parts[3])).astype(F32)
            mine = j < first
            total0 = total0 + jnp.where(mine, part, 0.0)
            total1 = total1 + jnp.where(mine, 0.0, part)
        at = pl.multiple_of(b * (2 * ROWS), 8)
        for t, total in enumerate((total0, total1)):
            for tile in range(6):
                i, h = divmod(tile, 2)
                sums_ref[pl.ds(at + t * ROWS + 8 * tile, 8), :] = total[i, :, h * C : (h + 1) * C]


def update_nodes(nodes_ref, sums_ref, first_ref, harm_sums_ref, weight_ref, squares_ref, combined_ref):
    squares_ref[...] = jnp.zeros((NODES, C), F32)

    def one(lm, degree, left):
        left = jnp.concatenate([left, harm_sums_ref[lm]], axis=1).astype(BF16)
        mixed = jnp.dot(left, weight_ref[degree], preferred_element_type=F32)
        cut = pl.ds(pl.multiple_of(lm * C, C), C)
        value = nodes_ref[:, cut].astype(F32) + mixed
        combined_ref[:, cut] = value
        squares_ref[...] += value * value

    one(0, 0, first_ref[...])

    @pl.loop(0, 12)
    def _(step):
        for n in range(4):
            lm = step * 4 + n + 1
            degree = 1
            for d in range(2, DEG):
                degree = degree + (lm >= d * d).astype(I32)
            one(lm, degree, sums_ref[pl.ds(lm - 1, NODES, stride=ROWS), :])


def layer_kernel(
    table_ref,
    gates_ref,
    harm_sums_ref,
    first_ref,
    slot_ref,
    mix_ref,
    harmonic_ref,
    update_ref,
    gain_ref,
    nodes_ref,
    out_hbm,
    slots,
    weight_ref,
    sums_ref,
    squares_ref,
    combined_ref,
    out_ref,
    slot_sem,
    out_sem,
):
    slot_copy = pltpu.make_async_copy(slot_ref, slots, slot_sem)
    slot_copy.start()
    for degree in range(DEG):
        both = jnp.concatenate([mix_ref[degree], harmonic_ref[...]], axis=0)
        weight_ref[degree] = jnp.dot(both, update_ref[degree], preferred_element_type=F32).astype(BF16)
    slot_copy.wait()
    sum_edges(slots, table_ref, gates_ref, sums_ref)
    update_nodes(nodes_ref, sums_ref, first_ref, harm_sums_ref, weight_ref, squares_ref, combined_ref)
    mean = jnp.sum(squares_ref[...], axis=1, keepdims=True) / FEAT
    squares_ref[...] = jnp.broadcast_to(lax.rsqrt(mean + norm_eps), (NODES, C))
    copies = []
    for c in range(PIECES):
        for lm in range(7 * c, 7 * c + 7, 2):
            pair = []
            for at in range(lm, min(lm + 2, 7 * c + 7)):
                degree = int(DEGREE_OF[at])
                pair.append(
                    combined_ref[:, at * C : (at + 1) * C]
                    * squares_ref[...]
                    * gain_ref[degree : degree + 1, :]
                )
            value = jnp.concatenate(pair, axis=1) if len(pair) == 2 else pair[0]
            out_ref[:, lm * C : (lm + len(pair)) * C] = value.astype(BF16)
        cut = pl.ds(c * PIECE, PIECE)
        copy = pltpu.make_async_copy(out_ref.at[:, cut], out_hbm.at[:, cut], out_sem.at[c])
        copy.start()
        copies.append(copy)
    for copy in copies:
        copy.wait()


VMEM = pl.BlockSpec(memory_space=pltpu.VMEM)
ANY = pl.BlockSpec(memory_space=pl.ANY)
HBM = pl.BlockSpec(memory_space=pltpu.HBM)


def gather(*arrays, peers, columns):
    return pl.pallas_call(
        functools.partial(gather_kernel, peers=peers, columns=columns),
        out_shape=(
            pltpu.VMEM(((TABLE + 1) * PARTS, 8, WIDE), BF16),
            pltpu.VMEM((LENGTHS * PARTS, 8, WIDE), BF16),
            pltpu.VMEM((COEF, NODES, C), F32),
            pltpu.VMEM((NODES, C), F32),
            pltpu.VMEM((BLOCKS, 2 * HALF), I32),
        ),
        in_specs=[HBM] * 9,
        out_specs=(VMEM,) * 5,
        scratch_shapes=[
            pltpu.VMEM((4, HALO), I32),
            pltpu.VMEM((1, BLOCKS - KEEP), I32),
            pltpu.VMEM((EB, BLOCKS), I32),
            pltpu.VMEM((EB, BLOCKS), I32),
            pltpu.VMEM((EB, BLOCKS), BF16),
            pltpu.VMEM((HID, RB), BF16),
            pltpu.VMEM((COEF, EB, BLOCKS), BF16),
            pltpu.VMEM((NODES, FEAT), BF16),
            pltpu.VMEM((HID, DEG * C), BF16),
            pltpu.VMEM((4 * HALO, FEAT), BF16),
            pltpu.VMEM((4 * HALO, FEAT), BF16),
            pltpu.VMEM((LENGTHS, DEG * C), F32),
            pltpu.VMEM((LENGTHS, C), BF16),
            pltpu.VMEM((16 * ROWS, C), F32),
            pltpu.VMEM((TABLE, C), BF16),
            pltpu.VMEM((BLOCKS, EB), I32),
            pltpu.VMEM((BLOCKS, EB), I32),
            pltpu.VMEM((BLOCKS, EB), I32),
            pltpu.VMEM((3, GROUPS, GE), I32),
            pltpu.VMEM((7, BLOCKS, EB), F32),
            pltpu.VMEM((COEF * GROUPS, GE), F32),
            pltpu.SemaphoreType.DMA((PIECES,)),
            pltpu.SemaphoreType.DMA((8,)),
            pltpu.SemaphoreType.DMA((4, PIECES)),
            pltpu.SemaphoreType.DMA((4, PIECES)),
        ],
        compiler_params=pltpu.CompilerParams(
            collective_id=0, has_side_effects=True, vmem_limit_bytes=GATHER_VMEM
        ),
        name="gather",
    )(*[pltpu.with_memory_space_constraint(a, pltpu.HBM) for a in arrays])


def layer(table, gates, harm_sums, first, slot, mix, harmonic, update, gain, nodes):
    return pl.pallas_call(
        layer_kernel,
        out_shape=jax.ShapeDtypeStruct((NODES, FEAT), BF16),
        in_specs=[VMEM] * 10,
        out_specs=ANY,
        scratch_shapes=[
            pltpu.SMEM((BLOCKS, 2 * HALF), I32),
            pltpu.VMEM((DEG, 2 * C, C), BF16),
            pltpu.VMEM((NODES * ROWS, C), F32),
            pltpu.VMEM((NODES, C), F32),
            pltpu.VMEM((NODES, FEAT), F32),
            pltpu.VMEM((NODES, FEAT), BF16),
            pltpu.SemaphoreType.DMA,
            pltpu.SemaphoreType.DMA((PIECES,)),
        ],
        compiler_params=pltpu.CompilerParams(vmem_limit_bytes=LAYER_VMEM),
        name="layer",
    )(table, gates, harm_sums, first, slot, mix, harmonic, update, gain, nodes)


GATHER_VMEM = 22 * 1024 * 1024
LAYER_VMEM = 26 * 1024 * 1024


def per_device(
    node_feats,
    halo_index,
    edge_source,
    edge_target,
    edge_length,
    edge_harmonics,
    block_peer,
    radial_in,
    radial_out,
    mix_weight,
    harmonic_weight,
    update_weight,
    norm_gain,
):
    gathered = gather(
        node_feats,
        halo_index[0],
        block_peer,
        edge_source.T,
        edge_target.T,
        edge_length.T,
        radial_in.T,
        radial_out,
        edge_harmonics.transpose(2, 1, 0),
        peers=lax.axis_size("gx"),
        columns=lax.axis_size("gy"),
    )
    return layer(*gathered, mix_weight, harmonic_weight, update_weight, norm_gain, node_feats)


def solution(mesh):
    split = ("gx", "gy")
    in_specs = (
        P(split, None),
        P(split, None, None),
        P(split, None),
        P(split, None),
        P(split, None),
        P(split, None, None),
        P(split, None),
        P(),
        P(),
        P(),
        P(),
        P(),
        P(),
    )
    return jax.shard_map(
        per_device, mesh=mesh, in_specs=in_specs, out_specs=P(split, None), check_vma=False
    )
```

```python
import functools

import jax
import jax.numpy as jnp
import numpy as np
from jax import lax
from jax.experimental import pallas as pl
from jax.experimental.pallas import tpu as pltpu
from jax.sharding import PartitionSpec as P

LMAX = 6
DEG = 7
COEF = 49
C = 128
HID = 600
RB = 128
FEAT = 6272
EB = 32
TB = 2
KEEP = 96
BLOCKS = 128
NODES = 256
HALO = 32
TABLE = NODES + 4 * HALO
GROUP = 8
GROUPS = BLOCKS // GROUP
GE = GROUP * EB
GN = GROUP * TB
LENGTHS = 384
ROWS = 48
CHUNK = 4
CHUNKS = EB // CHUNK + 1
SLOTS = CHUNK * CHUNKS
ZERO_ROW = TABLE

cutoff_radius = 6.0
norm_eps = 1e-06

F32 = jnp.float32
BF16 = jnp.bfloat16
I32 = jnp.int32

DEGREE_OF = np.repeat(np.arange(LMAX + 1), 2 * np.arange(LMAX + 1) + 1)
PARTS = 3
WIDE = 2 * C
LISTS = 80
STEP = 8
BAND = 32
PIECE = 7 * C
PIECES = FEAT // PIECE
MESH = pl.DeviceIdType.MESH


def length_index(length):
    r = length.astype(F32)
    f = jnp.where(
        r < 1.0,
        (r - 0.796875) * 256.0,
        jnp.where(
            r < 2.0,
            (r - 1.0) * 128.0 + 52.0,
            jnp.where(r < 4.0, (r - 2.0) * 64.0 + 180.0, (r - 4.0) * 32.0 + 308.0),
        ),
    )
    return f.astype(I32)


def length_of(i):
    return jnp.where(
        i < 52.0,
        0.796875 + i / 256.0,
        jnp.where(
            i < 180.0,
            1.0 + (i - 52.0) / 128.0,
            jnp.where(i < 308.0, 2.0 + (i - 180.0) / 64.0, 4.0 + (i - 308.0) / 32.0),
        ),
    )


def fill_gates(radial_in_ref, radial_out_ref, gate_ref, gate0_ref, table_ref):
    i = lax.broadcasted_iota(I32, (LENGTHS, RB), 0).astype(F32)
    r = length_of(i)
    k = lax.broadcasted_iota(I32, (LENGTHS, RB), 1).astype(F32)
    centers = cutoff_radius * (k + 0.5) / RB
    spread = 2.0 * cutoff_radius / RB
    along = length_of(lax.broadcasted_iota(I32, (8, LENGTHS), 1).astype(F32))
    envelope = (0.5 * (jnp.cos(jnp.pi * along / cutoff_radius) + 1.0)).T[:, :1]
    offsets = (r - centers) / spread
    basis = (jnp.exp(-0.5 * offsets * offsets) * envelope).astype(BF16)
    hidden = lax.dot_general(
        basis, radial_in_ref[...], (((1,), (1,)), ((), ())), preferred_element_type=F32
    )
    hidden = jax.nn.silu(hidden).astype(BF16)
    gate = jnp.dot(hidden, radial_out_ref[...], preferred_element_type=F32).astype(BF16)
    gate0_ref[...] = gate[:, :C]
    gate_ref[...] = gate.astype(F32)
    row = lax.broadcasted_iota(I32, (8, C), 0)

    @pl.loop(0, LENGTHS // 8)
    def _(g):
        rows = [gate_ref[pl.ds(g * 8, 8), d * C : (d + 1) * C] for d in range(DEG)]
        at = g * (8 * PARTS)
        for j in range(8):
            tiles = []
            for tile in range(6):
                first = int(DEGREE_OF[1 + 8 * tile])
                last = int(DEGREE_OF[8 + 8 * tile])
                value = jnp.broadcast_to(rows[first][j : j + 1], (8, C))
                if last != first:
                    split = last * last - (1 + 8 * tile)
                    value = jnp.where(
                        row < split, value, jnp.broadcast_to(rows[last][j : j + 1], (8, C))
                    )
                tiles.append(value)
            for i in range(3):
                table_ref[at + j * PARTS + i] = jnp.concatenate(
                    tiles[2 * i : 2 * i + 2], axis=1
                ).astype(BF16)


def spread_rows(source_ref, count, base, wide_ref, table_ref):
    @pl.loop(0, count // 16)
    def _(g):
        at = pl.multiple_of(g * 16, 16)
        for lm in range(1, COEF, 2):
            pair = source_ref[pl.ds(at, 16), lm * C : (lm + 2) * C].astype(F32)
            wide_ref[pl.ds(lm - 1, 16, stride=ROWS), :] = pair[:, :C]
            wide_ref[pl.ds(lm, 16, stride=ROWS), :] = pair[:, C:]
        to = (base + at) * PARTS
        for j in range(16):
            for i in range(3):
                low = j * ROWS + 16 * i
                table_ref[to + j * PARTS + i] = jnp.concatenate(
                    [wide_ref[low : low + 8, :], wide_ref[low + 8 : low + 16, :]], axis=1
                ).astype(BF16)


def column_of(row, size):
    diagonal = lax.broadcasted_iota(I32, (size, size), 0) == lax.broadcasted_iota(I32, (size, size), 1)
    return jnp.sum(jnp.where(diagonal, jnp.broadcast_to(row, (size, size)), 0), axis=1, keepdims=True)


def fill_lists(peer_ref, source_ref, target_ref, length_ref, peers, across_refs, slot_ref):
    peer = jnp.concatenate([jnp.zeros((1, KEEP), I32), peer_ref[...]], axis=1)
    target = jnp.where(peer < peers, target_ref[...], TB)
    source = source_ref[...]
    length = length_index(length_ref[...])
    for ref, value in zip(across_refs, (source, length, target)):
        ref[...] = value.T
    lower = (
        lax.broadcasted_iota(I32, (EB, EB), 0) > lax.broadcasted_iota(I32, (EB, EB), 1)
    ).astype(F32)
    zero = (target == 0).astype(F32)
    one = (target == 1).astype(F32)
    rank0 = jnp.dot(lower, zero, preferred_element_type=F32).astype(I32)
    rank1 = jnp.dot(lower, one, preferred_element_type=F32).astype(I32)
    slot = jnp.where(target == 0, rank0, jnp.where(target == 1, SLOTS - 1 - rank1, -1))
    relative = (source - ZERO_ROW) * PARTS
    length = length * PARTS
    count0 = jnp.sum(zero, axis=0, keepdims=True).astype(I32)
    rows = []
    for s in range(SLOTS):
        rows.append(jnp.sum(jnp.where(slot == s, relative, 0), axis=0, keepdims=True) + ZERO_ROW * PARTS)
    rows.append(lax.shift_right_logical(count0 + (CHUNK - 1), 2))
    for s in range(SLOTS):
        rows.append(jnp.sum(jnp.where(slot == s, length, 0), axis=0, keepdims=True))
    rows.append(jnp.zeros((LISTS - 2 * SLOTS - 1, BLOCKS), I32))
    slot_ref[...] = jnp.concatenate(rows, axis=0)


def by_group(ref):
    return jnp.concatenate([ref[pl.ds(b, GROUPS, stride=GROUP), :] for b in range(GROUP)], axis=1)


def transposed(x):
    rows = x.shape[1]
    identity = (
        lax.broadcasted_iota(I32, (rows, rows), 0) == lax.broadcasted_iota(I32, (rows, rows), 1)
    ).astype(F32).astype(BF16)
    return lax.dot_general(identity, x, (((1,), (1,)), ((), ())), preferred_element_type=F32)


def turn_harmonics(
    across_refs, harm_ref, scalars_ref, gate0_ref, turned_ref, rows_ref, harm_rows_ref, zeroth_ref
):
    for n, ref in enumerate(across_refs):
        rows_ref[n] = by_group(ref)

    @pl.loop(0, COEF // 7)
    def _(step):
        for n in range(7):
            turned_ref[n] = harm_ref[step * 7 + n].astype(F32).T
            at = pl.multiple_of((step * 7 + n) * GROUPS, GROUPS)
            harm_rows_ref[pl.ds(at, GROUPS), :] = by_group(turned_ref.at[n])

    zeroth_ref[1] = transposed(gate0_ref[...]).astype(BF16)


def harmonic_sums(g, wanted, rows_ref, harm_rows_ref, zeroth_ref, harm_sums_ref, first_ref):
    across = (((1,), (1,)), ((), ()))
    row = lax.broadcasted_iota(I32, (TABLE, GE), 0)
    pick = (rows_ref[0, pl.ds(g, 1), :] == row).astype(F32).astype(BF16)
    scalar = jnp.dot(zeroth_ref[0], pick, preferred_element_type=F32).astype(BF16)
    pick = (rows_ref[1, pl.ds(g, 1), :] == row).astype(F32).astype(BF16)
    gate = jnp.dot(zeroth_ref[1], pick, preferred_element_type=F32).astype(BF16)
    mask = (rows_ref[2, pl.ds(g, 1), :] == wanted).astype(F32)
    at = pl.multiple_of(g * GN, GN)
    first_ref[pl.ds(at, GN), :] = lax.dot_general(
        mask.astype(BF16), scalar * gate, across, preferred_element_type=F32
    )
    left = jnp.concatenate(
        [(harm_rows_ref[pl.ds(lm * GROUPS + g, 1), :] * mask).astype(BF16) for lm in range(COEF)],
        axis=0,
    )
    right = lax.dot_general(left, scalar, across, preferred_element_type=F32)
    for lm in range(COEF):
        harm_sums_ref[lm, pl.ds(at, GN), :] = right[lm * GN : (lm + 1) * GN]


def gather_kernel(
    nodes_hbm,
    halo_hbm,
    peer_hbm,
    source_hbm,
    target_hbm,
    length_hbm,
    radial_in_hbm,
    radial_out_hbm,
    harm_hbm,
    mix_hbm,
    harmonic_hbm,
    update_hbm,
    table_ref,
    gates_ref,
    rows_ref,
    harm_rows_ref,
    zeroth_ref,
    slot_ref,
    weight_ref,
    halo_ref,
    peer_ref,
    source_ref,
    target_ref,
    length_ref,
    radial_in_ref,
    harm_ref,
    mix_ref,
    harmonic_ref,
    update_ref,
    nodes_ref,
    radial_out_ref,
    send_ref,
    arrived_ref,
    gate_ref,
    gate0_ref,
    wide_ref,
    scalars_ref,
    source_across_ref,
    length_across_ref,
    target_across_ref,
    turned_ref,
    load_sem,
    other_sem,
    send_sem,
    recv_sem,
    peers,
    columns,
):
    p, q = lax.axis_index("gx"), lax.axis_index("gy")
    ahead, behind = lax.rem(p + 1, peers), lax.rem(p + peers - 1, peers)
    above, below = lax.rem(q + 1, columns), lax.rem(q + columns - 1, columns)
    neighbours = ((ahead, q), (behind, q), (p, above), (p, below))

    smalls = []
    for n, (source, target) in enumerate(
        (
            (halo_hbm, halo_ref),
            (peer_hbm, peer_ref),
            (source_hbm, source_ref),
            (target_hbm, target_ref),
            (length_hbm, length_ref),
            (radial_in_hbm, radial_in_ref),
            (radial_out_hbm, radial_out_ref),
            (harm_hbm, harm_ref),
            (mix_hbm, mix_ref),
            (harmonic_hbm, harmonic_ref),
            (update_hbm, update_ref),
        )
    ):
        smalls.append(pltpu.make_async_copy(source, target, other_sem.at[n]))
    smalls[0].start()
    loads = []
    for c in range(PIECES):
        cut = pl.ds(c * PIECE, PIECE)
        load = pltpu.make_async_copy(nodes_hbm.at[:, cut], nodes_ref.at[:, cut], load_sem.at[c])
        load.start()
        loads.append(load)
    for load in smalls[1:]:
        load.start()

    barrier = pltpu.get_barrier_semaphore()
    for neighbour in neighbours:
        pl.semaphore_signal(barrier, inc=1, device_id=neighbour, device_id_type=MESH)

    smalls[0].wait()
    index = column_of(jnp.concatenate([halo_ref[k : k + 1, :] for k in range(4)], axis=1), 4 * HALO)
    pick = (lax.broadcasted_iota(I32, (4 * HALO, NODES), 1) == index).astype(F32).astype(BF16)
    pl.semaphore_wait(barrier, 4)
    copies = []
    for c in range(PIECES):
        loads[c].wait()
        cut = pl.ds(c * PIECE, PIECE)
        send_ref[:, cut] = jnp.dot(pick, nodes_ref[:, cut], preferred_element_type=F32).astype(BF16)
        for k in (2, 3, 0, 1):
            part = pl.ds(k * HALO, HALO)
            copy = pltpu.make_async_remote_copy(
                src_ref=send_ref.at[part, cut],
                dst_ref=arrived_ref.at[part, cut],
                send_sem=send_sem.at[k, c],
                recv_sem=recv_sem.at[k, c],
                device_id=neighbours[k],
                device_id_type=MESH,
            )
            copy.start()
            copies.append(copy)

    for load in smalls[1:5]:
        load.wait()
    across_refs = (source_across_ref, length_across_ref, target_across_ref)
    fill_lists(peer_ref, source_ref, target_ref, length_ref, peers, across_refs, slot_ref)
    smalls[5].wait()
    smalls[6].wait()
    fill_gates(radial_in_ref, radial_out_ref, gate_ref, gate0_ref, gates_ref)
    spread_rows(nodes_ref, NODES, 0, wide_ref, table_ref)
    table_ref[ZERO_ROW * PARTS :] = jnp.zeros((PARTS, 8, WIDE), BF16)
    smalls[7].wait()
    turn_harmonics(
        across_refs, harm_ref, scalars_ref, gate0_ref, turned_ref, rows_ref, harm_rows_ref, zeroth_ref
    )
    for load in smalls[8:]:
        load.wait()
    for degree in range(DEG):
        both = jnp.concatenate([mix_ref[degree], harmonic_ref[...]], axis=0)
        weight_ref[degree] = jnp.dot(both, update_ref[degree], preferred_element_type=F32).astype(BF16)
    for copy in copies:
        copy.wait_recv()
    spread_rows(arrived_ref, 4 * HALO, NODES, wide_ref, table_ref)
    scalars_ref[:NODES, :] = nodes_ref[:, :C]
    scalars_ref[NODES:, :] = arrived_ref[:, :C]
    zeroth_ref[0] = transposed(scalars_ref[...]).astype(BF16)
    for copy in copies:
        copy.wait_send()


def sum_edges(b, slots, table_ref, gates_ref, sums_ref):
    first = slots[SLOTS][b]
    total0 = jnp.zeros((PARTS, 8, WIDE), F32)
    running = jnp.zeros((PARTS, 8, WIDE), F32)
    for j in range(CHUNKS):
        parts = []
        for k in range(CHUNK):
            at = j * CHUNK + k
            parts.append(
                table_ref[pl.ds(slots[at][b], PARTS)] * gates_ref[pl.ds(slots[SLOTS + 1 + at][b], PARTS)]
            )
        part = ((parts[0] + parts[1]) + (parts[2] + parts[3])).astype(F32)
        running = running + part
        total0 = jnp.where(j < first, running, total0)
    at = pl.multiple_of(b * (2 * ROWS), 8)
    for t, total in enumerate((total0, running - total0)):
        for tile in range(6):
            i, h = divmod(tile, 2)
            sums_ref[pl.ds(at + t * ROWS + 8 * tile, 8), :] = total[i, :, h * C : (h + 1) * C]


def sum_blocks(slots, rows_ref, harm_rows_ref, zeroth_ref, table_ref, gates_ref, sums_ref, harm_sums_ref, first_ref):
    node = lax.broadcasted_iota(I32, (GN, GE), 0)
    edge = lax.broadcasted_iota(I32, (GN, GE), 1)
    same_block = lax.shift_right_logical(node, 1) == lax.shift_right_logical(edge, 5)
    wanted = jnp.where(same_block, lax.bitwise_and(node, 1), -1)

    @pl.loop(0, GROUPS)
    def _(g):
        harmonic_sums(g, wanted, rows_ref, harm_rows_ref, zeroth_ref, harm_sums_ref, first_ref)
        for n in range(GROUP):
            sum_edges(g * GROUP + n, slots, table_ref, gates_ref, sums_ref)


def update_nodes(nodes_ref, sums_ref, first_ref, harm_sums_ref, weight_ref, squares_ref, combined_ref):
    def one(lm, degree, left):
        left = jnp.concatenate([left, harm_sums_ref[lm]], axis=1).astype(BF16)
        mixed = jnp.dot(left, weight_ref[degree], preferred_element_type=F32)
        cut = pl.ds(pl.multiple_of(lm * C, C), C)
        value = nodes_ref[:, cut].astype(F32) + mixed
        combined_ref[:, cut] = value
        return value * value

    squares_ref[...] = one(0, 0, first_ref[...])

    @pl.loop(0, 48 // STEP)
    def _(step):
        squares = None
        for n in range(STEP):
            lm = step * STEP + n + 1
            degree = 1
            for d in range(2, DEG):
                degree = degree + (lm >= d * d).astype(I32)
            square = one(lm, degree, sums_ref[pl.ds(lm - 1, NODES, stride=ROWS), :])
            squares = square if squares is None else squares + square
        squares_ref[...] += squares


def store_nodes(squares_ref, gain_ref, combined_ref, out_ref, out_hbm, out_sem):
    mean = jnp.sum(squares_ref[...], axis=1, keepdims=True) / FEAT
    squares_ref[...] = jnp.broadcast_to(lax.rsqrt(mean + norm_eps), (NODES, C))

    def copy(n):
        cut = pl.ds(pl.multiple_of(n * BAND, BAND), BAND)
        return pltpu.make_async_copy(out_ref.at[cut], out_hbm.at[cut], out_sem.at[n])

    @pl.loop(0, NODES // BAND)
    def _(n):
        cut = pl.ds(pl.multiple_of(n * BAND, BAND), BAND)
        inverse = squares_ref[cut, :]
        for lm in range(0, COEF, 2):
            pair = []
            for at in range(lm, min(lm + 2, COEF)):
                degree = int(DEGREE_OF[at])
                pair.append(
                    combined_ref[cut, at * C : (at + 1) * C] * inverse * gain_ref[degree : degree + 1, :]
                )
            value = jnp.concatenate(pair, axis=1) if len(pair) == 2 else pair[0]
            out_ref[cut, lm * C : (lm + len(pair)) * C] = value.astype(BF16)
        copy(n).start()

    for n in range(NODES // BAND):
        copy(n).wait()


def layer_kernel(
    table_ref,
    gates_ref,
    rows_ref,
    harm_rows_ref,
    zeroth_ref,
    slot_ref,
    weight_ref,
    gain_ref,
    nodes_ref,
    out_hbm,
    sums_ref,
    harm_sums_ref,
    first_ref,
    squares_ref,
    combined_ref,
    out_ref,
    slot_sem,
    out_sem,
    *slots,
):
    slot_copies = []
    for n, slot in enumerate(slots):
        copy = pltpu.make_async_copy(slot_ref.at[n], slot, slot_sem.at[n])
        copy.start()
        slot_copies.append(copy)
    for copy in slot_copies:
        copy.wait()
    sum_blocks(
        slots, rows_ref, harm_rows_ref, zeroth_ref, table_ref, gates_ref, sums_ref, harm_sums_ref, first_ref
    )
    update_nodes(nodes_ref, sums_ref, first_ref, harm_sums_ref, weight_ref, squares_ref, combined_ref)
    store_nodes(squares_ref, gain_ref, combined_ref, out_ref, out_hbm, out_sem)


VMEM = pl.BlockSpec(memory_space=pltpu.VMEM)
ANY = pl.BlockSpec(memory_space=pl.ANY)
HBM = pl.BlockSpec(memory_space=pltpu.HBM)


def gather(*arrays, peers, columns):
    return pl.pallas_call(
        functools.partial(gather_kernel, peers=peers, columns=columns),
        out_shape=(
            pltpu.VMEM(((TABLE + 1) * PARTS, 8, WIDE), BF16),
            pltpu.VMEM((LENGTHS * PARTS, 8, WIDE), BF16),
            pltpu.VMEM((3, GROUPS, GE), I32),
            pltpu.VMEM((COEF * GROUPS, GE), F32),
            pltpu.VMEM((2, C, TABLE), BF16),
            pltpu.VMEM((LISTS, BLOCKS), I32),
            pltpu.VMEM((DEG, 2 * C, C), BF16),
        ),
        in_specs=[HBM] * 12,
        out_specs=(VMEM,) * 7,
        scratch_shapes=[
            pltpu.VMEM((4, HALO), I32),
            pltpu.VMEM((1, BLOCKS - KEEP), I32),
            pltpu.VMEM((EB, BLOCKS), I32),
            pltpu.VMEM((EB, BLOCKS), I32),
            pltpu.VMEM((EB, BLOCKS), BF16),
            pltpu.VMEM((HID, RB), BF16),
            pltpu.VMEM((COEF, EB, BLOCKS), BF16),
            pltpu.VMEM((DEG, C, C), BF16),
            pltpu.VMEM((C, C), BF16),
            pltpu.VMEM((DEG, C, C), BF16),
            pltpu.VMEM((NODES, FEAT), BF16),
            pltpu.VMEM((HID, DEG * C), BF16),
            pltpu.VMEM((4 * HALO, FEAT), BF16),
            pltpu.VMEM((4 * HALO, FEAT), BF16),
            pltpu.VMEM((LENGTHS, DEG * C), F32),
            pltpu.VMEM((LENGTHS, C), BF16),
            pltpu.VMEM((16 * ROWS, C), F32),
            pltpu.VMEM((TABLE, C), BF16),
            pltpu.VMEM((BLOCKS, EB), I32),
            pltpu.VMEM((BLOCKS, EB), I32),
            pltpu.VMEM((BLOCKS, EB), I32),
            pltpu.VMEM((7, BLOCKS, EB), F32),
            pltpu.SemaphoreType.DMA((PIECES,)),
            pltpu.SemaphoreType.DMA((11,)),
            pltpu.SemaphoreType.DMA((4, PIECES)),
            pltpu.SemaphoreType.DMA((4, PIECES)),
        ],
        compiler_params=pltpu.CompilerParams(
            collective_id=0, has_side_effects=True, vmem_limit_bytes=GATHER_VMEM
        ),
        name="gather",
    )(*[pltpu.with_memory_space_constraint(a, pltpu.HBM) for a in arrays])


def layer(*arrays):
    return pl.pallas_call(
        layer_kernel,
        out_shape=jax.ShapeDtypeStruct((NODES, FEAT), BF16),
        in_specs=[VMEM] * len(arrays),
        out_specs=ANY,
        scratch_shapes=[
            pltpu.VMEM((NODES * ROWS, C), F32),
            pltpu.VMEM((COEF, NODES, C), F32),
            pltpu.VMEM((NODES, C), F32),
            pltpu.VMEM((NODES, C), F32),
            pltpu.VMEM((NODES, FEAT), F32),
            pltpu.VMEM((NODES, FEAT), BF16),
            pltpu.SemaphoreType.DMA((2 * SLOTS + 1,)),
            pltpu.SemaphoreType.DMA((NODES // BAND,)),
        ]
        + [pltpu.SMEM((BLOCKS,), I32)] * (2 * SLOTS + 1),
        compiler_params=pltpu.CompilerParams(vmem_limit_bytes=LAYER_VMEM),
        name="layer",
    )(*arrays)


GATHER_VMEM = 22 * 1024 * 1024
LAYER_VMEM = 30 * 1024 * 1024


def per_device(
    node_feats,
    halo_index,
    edge_source,
    edge_target,
    edge_length,
    edge_harmonics,
    block_peer,
    radial_in,
    radial_out,
    mix_weight,
    harmonic_weight,
    update_weight,
    norm_gain,
):
    gathered = gather(
        node_feats,
        halo_index[0],
        block_peer,
        edge_source.T,
        edge_target.T,
        edge_length.T,
        radial_in.T,
        radial_out,
        edge_harmonics.transpose(2, 1, 0),
        mix_weight,
        harmonic_weight,
        update_weight,
        peers=lax.axis_size("gx"),
        columns=lax.axis_size("gy"),
    )
    return layer(*gathered, norm_gain, node_feats)


def solution(mesh):
    split = ("gx", "gy")
    in_specs = (
        P(split, None),
        P(split, None, None),
        P(split, None),
        P(split, None),
        P(split, None),
        P(split, None, None),
        P(split, None),
        P(),
        P(),
        P(),
        P(),
        P(),
        P(),
    )
    return jax.shard_map(
        per_device, mesh=mesh, in_specs=in_specs, out_specs=P(split, None), check_vma=False
    )
```

```python
import functools

import jax
import jax.numpy as jnp
import numpy as np
from jax import lax
from jax.experimental import pallas as pl
from jax.experimental.pallas import tpu as pltpu
from jax.sharding import PartitionSpec as P

LMAX = 6
DEG = 7
COEF = 49
C = 128
HID = 600
RB = 128
FEAT = 6272
EB = 32
TB = 2
KEEP = 96
BLOCKS = 128
NODES = 256
HALO = 32
TABLE = NODES + 4 * HALO
GROUP = 8
GROUPS = BLOCKS // GROUP
GE = GROUP * EB
GN = GROUP * TB
LENGTHS = 384
ROWS = 49
CHUNK = 4
CHUNKS = BLOCKS * (EB // CHUNK + 1)
WORK = 16
QUARTERS = WORK // CHUNK
STEPS = CHUNKS // QUARTERS
LANES = 384
LISTS = 2 * WORK + QUARTERS + 1
FIXED = 8

cutoff_radius = 6.0
norm_eps = 1e-06

F32 = jnp.float32
BF16 = jnp.bfloat16
I32 = jnp.int32

DEGREE_OF = np.repeat(np.arange(LMAX + 1), 2 * np.arange(LMAX + 1) + 1)
PARTS = 3
WIDE = 2 * C
STEP = 8
BAND = 32
PIECE = 7 * C
PIECES = FEAT // PIECE
MESH = pl.DeviceIdType.MESH


def length_index(length):
    r = length.astype(F32)
    f = jnp.where(
        r < 1.0,
        (r - 0.796875) * 256.0,
        jnp.where(
            r < 2.0,
            (r - 1.0) * 128.0 + 52.0,
            jnp.where(r < 4.0, (r - 2.0) * 64.0 + 180.0, (r - 4.0) * 32.0 + 308.0),
        ),
    )
    return f.astype(I32)


def length_of(i):
    return jnp.where(
        i < 52.0,
        0.796875 + i / 256.0,
        jnp.where(
            i < 180.0,
            1.0 + (i - 52.0) / 128.0,
            jnp.where(i < 308.0, 2.0 + (i - 180.0) / 64.0, 4.0 + (i - 308.0) / 32.0),
        ),
    )


def fill_gates(radial_in_ref, radial_out_ref, gate_ref, gate0_ref, table_ref):
    i = lax.broadcasted_iota(I32, (LENGTHS, RB), 0).astype(F32)
    r = length_of(i)
    k = lax.broadcasted_iota(I32, (LENGTHS, RB), 1).astype(F32)
    centers = cutoff_radius * (k + 0.5) / RB
    spread = 2.0 * cutoff_radius / RB
    along = length_of(lax.broadcasted_iota(I32, (8, LENGTHS), 1).astype(F32))
    envelope = (0.5 * (jnp.cos(jnp.pi * along / cutoff_radius) + 1.0)).T[:, :1]
    offsets = (r - centers) / spread
    basis = (jnp.exp(-0.5 * offsets * offsets) * envelope).astype(BF16)
    hidden = lax.dot_general(
        basis, radial_in_ref[...], (((1,), (1,)), ((), ())), preferred_element_type=F32
    )
    hidden = jax.nn.silu(hidden).astype(BF16)
    gate = jnp.dot(hidden, radial_out_ref[...], preferred_element_type=F32).astype(BF16)
    gate0_ref[...] = gate[:, :C]
    gate_ref[...] = gate.astype(F32)
    row = lax.broadcasted_iota(I32, (8, C), 0)

    @pl.loop(0, LENGTHS // 8)
    def _(g):
        rows = [gate_ref[pl.ds(g * 8, 8), d * C : (d + 1) * C] for d in range(DEG)]
        at = g * (8 * PARTS)
        for j in range(8):
            tiles = []
            for tile in range(6):
                first = int(DEGREE_OF[1 + 8 * tile])
                last = int(DEGREE_OF[8 + 8 * tile])
                value = jnp.broadcast_to(rows[first][j : j + 1], (8, C))
                if last != first:
                    split = last * last - (1 + 8 * tile)
                    value = jnp.where(
                        row < split, value, jnp.broadcast_to(rows[last][j : j + 1], (8, C))
                    )
                tiles.append(value)
            for i in range(3):
                table_ref[at + j * PARTS + i] = jnp.concatenate(
                    tiles[2 * i : 2 * i + 2], axis=1
                ).astype(BF16)


def spread_rows(source_ref, count, base, wide_ref, table_ref):
    @pl.loop(0, count // 16)
    def _(g):
        at = pl.multiple_of(g * 16, 16)
        for lm in range(1, COEF, 2):
            pair = source_ref[pl.ds(at, 16), lm * C : (lm + 2) * C].astype(F32)
            wide_ref[pl.ds(lm - 1, 16, stride=ROWS), :] = pair[:, :C]
            wide_ref[pl.ds(lm, 16, stride=ROWS), :] = pair[:, C:]
        to = (base + at) * PARTS
        for j in range(16):
            for i in range(3):
                low = j * ROWS + 16 * i
                table_ref[to + j * PARTS + i] = jnp.concatenate(
                    [wide_ref[low : low + 8, :], wide_ref[low + 8 : low + 16, :]], axis=1
                ).astype(BF16)


def column_of(row, size):
    diagonal = lax.broadcasted_iota(I32, (size, size), 0) == lax.broadcasted_iota(I32, (size, size), 1)
    return jnp.sum(jnp.where(diagonal, jnp.broadcast_to(row, (size, size)), 0), axis=1, keepdims=True)


def fill_lists(
    peer_ref, source_ref, target_ref, length_ref, peers, across_refs, place_ref, list_ref, slot_ref
):
    peer = jnp.concatenate([jnp.zeros((1, KEEP), I32), peer_ref[...]], axis=1)
    target = jnp.where(peer < peers, target_ref[...], TB)
    source = source_ref[...]
    length = length_index(length_ref[...])
    for ref, value in zip(across_refs, (source, length, target)):
        ref[...] = value.T
    lower = (
        lax.broadcasted_iota(I32, (EB, EB), 0) > lax.broadcasted_iota(I32, (EB, EB), 1)
    ).astype(F32)
    zero = (target == 0).astype(F32)
    one = (target == 1).astype(F32)
    rank0 = jnp.dot(lower, zero, preferred_element_type=F32).astype(I32)
    rank1 = jnp.dot(lower, one, preferred_element_type=F32).astype(I32)

    def chunks(mask):
        count = jnp.sum(mask, axis=0, keepdims=True).astype(I32)
        return jnp.maximum(lax.shift_right_logical(count + (CHUNK - 1), 2), 1)

    chunks0, chunks1 = chunks(zero), chunks(one)
    before = (
        lax.broadcasted_iota(I32, (BLOCKS, BLOCKS), 0) < lax.broadcasted_iota(I32, (BLOCKS, BLOCKS), 1)
    ).astype(F32)
    each = jnp.broadcast_to((chunks0 + chunks1).astype(F32), (8, BLOCKS))
    start = jnp.dot(each, before, preferred_element_type=F32).astype(I32)
    start0 = start[:1]
    start1 = start0 + chunks0
    place = jnp.where(target == 0, start0 * CHUNK + rank0, start1 * CHUNK + rank1)
    place = jnp.where(target < TB, place, -1)
    source = source + 1
    for n, value in enumerate(
        (
            lax.bitwise_and(place, WORK - 1),
            lax.shift_right_arithmetic(place, 4),
            lax.shift_right_logical(source, 8),
            lax.bitwise_and(source, 255),
            lax.shift_right_logical(length, 8),
            lax.bitwise_and(length, 255),
        )
    ):
        place_ref[n] = value
    list_ref[...] = jnp.zeros((4 * WORK, LANES), F32)

    @pl.loop(0, EB // 4)
    def _(step):
        column = lax.broadcasted_iota(I32, (LANES, BLOCKS), 0)
        lane = lax.broadcasted_iota(I32, (WORK, BLOCKS), 0)
        total = None
        for half in range(2):
            lefts, rights = [], []
            for n in range(2):
                e = step * 4 + half * 2 + n
                row = [place_ref[m, pl.ds(e, 1), :] for m in range(6)]
                mine = lane == row[0]
                lefts.append(
                    jnp.concatenate([jnp.where(mine, row[m], 0) for m in range(2, 6)], axis=0)
                    .astype(F32)
                    .astype(BF16)
                )
                rights.append((column == row[1]).astype(F32).astype(BF16))
            product = lax.dot_general(
                jnp.concatenate(lefts, axis=1),
                jnp.concatenate(rights, axis=1),
                (((1,), (1,)), ((), ())),
                preferred_element_type=F32,
            )
            total = product if total is None else total + product
        list_ref[...] += total

    found = list_ref[...].astype(I32)
    slot_ref[:WORK, :] = (found[:WORK] * 256 + found[WORK : 2 * WORK]) * PARTS
    slot_ref[WORK : 2 * WORK, :] = (found[2 * WORK : 3 * WORK] * 256 + found[3 * WORK :]) * PARTS
    starts = jnp.concatenate([start0, start1, jnp.zeros((6, BLOCKS), I32)], axis=0).T
    count = (start1 + chunks1)[:, BLOCKS - 1 :]
    for q in range(QUARTERS):
        chunk = lax.broadcasted_iota(I32, (BLOCKS, LANES), 1) * QUARTERS + q
        reached = jnp.zeros((1, LANES), I32)
        opened = jnp.zeros((1, LANES), I32)
        for t in range(TB):
            column = starts[:, t : t + 1]
            reached = reached + jnp.sum((column <= chunk).astype(I32), axis=0, keepdims=True)
            opened = opened + jnp.sum((column == chunk).astype(I32), axis=0, keepdims=True)
        node = jnp.where(chunk[:1] < count, reached - 1, NODES)
        slot_ref[2 * WORK + q : 2 * WORK + q + 1, :] = node * (2 * ROWS) + opened
    slot_ref[LISTS - 1 : LISTS, :] = jnp.broadcast_to(
        lax.shift_right_logical(count + (2 * QUARTERS - 1), 3), (1, LANES)
    )


def by_group(ref):
    return jnp.concatenate([ref[pl.ds(b, GROUPS, stride=GROUP), :] for b in range(GROUP)], axis=1)


def transposed(x):
    rows = x.shape[1]
    identity = (
        lax.broadcasted_iota(I32, (rows, rows), 0) == lax.broadcasted_iota(I32, (rows, rows), 1)
    ).astype(F32).astype(BF16)
    return lax.dot_general(identity, x, (((1,), (1,)), ((), ())), preferred_element_type=F32)


def turn_harmonics(
    across_refs, harm_ref, scalars_ref, gate0_ref, turned_ref, rows_ref, harm_rows_ref, zeroth_ref
):
    for n, ref in enumerate(across_refs):
        rows_ref[n] = by_group(ref)

    @pl.loop(0, COEF // 7)
    def _(step):
        for n in range(7):
            turned_ref[n] = harm_ref[step * 7 + n].astype(F32).T
            at = pl.multiple_of((step * 7 + n) * GROUPS, GROUPS)
            harm_rows_ref[pl.ds(at, GROUPS), :] = by_group(turned_ref.at[n])

    zeroth_ref[1] = transposed(gate0_ref[...]).astype(BF16)


def harmonic_sums(g, wanted, rows_ref, harm_rows_ref, zeroth_ref, harm_sums_ref, first_ref):
    across = (((1,), (1,)), ((), ()))
    row = lax.broadcasted_iota(I32, (TABLE, GE), 0)
    pick = (rows_ref[0, pl.ds(g, 1), :] == row).astype(F32).astype(BF16)
    scalar = jnp.dot(zeroth_ref[0], pick, preferred_element_type=F32).astype(BF16)
    pick = (rows_ref[1, pl.ds(g, 1), :] == row).astype(F32).astype(BF16)
    gate = jnp.dot(zeroth_ref[1], pick, preferred_element_type=F32).astype(BF16)
    mask = (rows_ref[2, pl.ds(g, 1), :] == wanted).astype(F32)
    at = pl.multiple_of(g * GN, GN)
    first_ref[pl.ds(at, GN), :] = lax.dot_general(
        mask.astype(BF16), scalar * gate, across, preferred_element_type=F32
    )
    left = jnp.concatenate(
        [(harm_rows_ref[pl.ds(lm * GROUPS + g, 1), :] * mask).astype(BF16) for lm in range(COEF)],
        axis=0,
    )
    right = lax.dot_general(left, scalar, across, preferred_element_type=F32)
    for lm in range(COEF):
        harm_sums_ref[lm, pl.ds(at, GN), :] = right[lm * GN : (lm + 1) * GN]


def gather_kernel(
    nodes_hbm,
    halo_hbm,
    peer_hbm,
    source_hbm,
    target_hbm,
    length_hbm,
    radial_in_hbm,
    radial_out_hbm,
    harm_hbm,
    mix_hbm,
    harmonic_hbm,
    update_hbm,
    table_ref,
    gates_ref,
    rows_ref,
    harm_rows_ref,
    zeroth_ref,
    slot_ref,
    weight_ref,
    halo_ref,
    peer_ref,
    source_ref,
    target_ref,
    length_ref,
    radial_in_ref,
    harm_ref,
    mix_ref,
    harmonic_ref,
    update_ref,
    nodes_ref,
    radial_out_ref,
    send_ref,
    arrived_ref,
    gate_ref,
    gate0_ref,
    wide_ref,
    scalars_ref,
    source_across_ref,
    length_across_ref,
    target_across_ref,
    turned_ref,
    place_ref,
    list_ref,
    load_sem,
    other_sem,
    send_sem,
    recv_sem,
    peers,
    columns,
):
    p, q = lax.axis_index("gx"), lax.axis_index("gy")
    ahead, behind = lax.rem(p + 1, peers), lax.rem(p + peers - 1, peers)
    above, below = lax.rem(q + 1, columns), lax.rem(q + columns - 1, columns)
    neighbours = ((ahead, q), (behind, q), (p, above), (p, below))

    smalls = []
    for n, (source, target) in enumerate(
        (
            (halo_hbm, halo_ref),
            (peer_hbm, peer_ref),
            (source_hbm, source_ref),
            (target_hbm, target_ref),
            (length_hbm, length_ref),
            (radial_in_hbm, radial_in_ref),
            (radial_out_hbm, radial_out_ref),
            (harm_hbm, harm_ref),
            (mix_hbm, mix_ref),
            (harmonic_hbm, harmonic_ref),
            (update_hbm, update_ref),
        )
    ):
        smalls.append(pltpu.make_async_copy(source, target, other_sem.at[n]))
    smalls[0].start()
    loads = []
    for c in range(PIECES):
        cut = pl.ds(c * PIECE, PIECE)
        load = pltpu.make_async_copy(nodes_hbm.at[:, cut], nodes_ref.at[:, cut], load_sem.at[c])
        load.start()
        loads.append(load)
    for load in smalls[1:]:
        load.start()

    barrier = pltpu.get_barrier_semaphore()
    for neighbour in neighbours:
        pl.semaphore_signal(barrier, inc=1, device_id=neighbour, device_id_type=MESH)

    smalls[0].wait()
    index = column_of(jnp.concatenate([halo_ref[k : k + 1, :] for k in range(4)], axis=1), 4 * HALO)
    pick = (lax.broadcasted_iota(I32, (4 * HALO, NODES), 1) == index).astype(F32).astype(BF16)
    pl.semaphore_wait(barrier, 4)
    copies = []
    for c in range(PIECES):
        loads[c].wait()
        cut = pl.ds(c * PIECE, PIECE)
        send_ref[:, cut] = jnp.dot(pick, nodes_ref[:, cut], preferred_element_type=F32).astype(BF16)
        for k in (2, 3, 0, 1):
            part = pl.ds(k * HALO, HALO)
            copy = pltpu.make_async_remote_copy(
                src_ref=send_ref.at[part, cut],
                dst_ref=arrived_ref.at[part, cut],
                send_sem=send_sem.at[k, c],
                recv_sem=recv_sem.at[k, c],
                device_id=neighbours[k],
                device_id_type=MESH,
            )
            copy.start()
            copies.append(copy)

    for load in smalls[1:5]:
        load.wait()
    across_refs = (source_across_ref, length_across_ref, target_across_ref)
    fill_lists(
        peer_ref,
        source_ref,
        target_ref,
        length_ref,
        peers,
        across_refs,
        place_ref,
        list_ref,
        slot_ref,
    )
    smalls[5].wait()
    smalls[6].wait()
    fill_gates(radial_in_ref, radial_out_ref, gate_ref, gate0_ref, gates_ref)
    spread_rows(nodes_ref, NODES, 1, wide_ref, table_ref)
    table_ref[:PARTS] = jnp.zeros((PARTS, 8, WIDE), BF16)
    smalls[7].wait()
    turn_harmonics(
        across_refs, harm_ref, scalars_ref, gate0_ref, turned_ref, rows_ref, harm_rows_ref, zeroth_ref
    )
    for load in smalls[8:]:
        load.wait()
    for degree in range(DEG):
        both = jnp.concatenate([mix_ref[degree], harmonic_ref[...]], axis=0)
        weight_ref[degree] = jnp.dot(both, update_ref[degree], preferred_element_type=F32).astype(BF16)
    for copy in copies:
        copy.wait_recv()
    spread_rows(arrived_ref, 4 * HALO, NODES + 1, wide_ref, table_ref)
    scalars_ref[:NODES, :] = nodes_ref[:, :C]
    scalars_ref[NODES:, :] = arrived_ref[:, :C]
    zeroth_ref[0] = transposed(scalars_ref[...]).astype(BF16)
    for copy in copies:
        copy.wait_send()


def sum_edges(step, total, slots, table_ref, gates_ref, sums_ref):
    for q in range(QUARTERS):
        parts = []
        for k in range(q * CHUNK, (q + 1) * CHUNK):
            parts.append(
                table_ref[pl.ds(slots[k][step], PARTS)] * gates_ref[pl.ds(slots[WORK + k][step], PARTS)]
            )
        part = ((parts[0] + parts[1]) + (parts[2] + parts[3])).astype(F32)
        word = slots[2 * WORK + q][step]
        total = jnp.where(lax.bitwise_and(word, 1) == 1, part, total + part)
        at = lax.shift_right_logical(word, 1)
        for tile in range(6):
            i, h = divmod(tile, 2)
            sums_ref[pl.ds(at + 8 * tile, 8), :] = total[i, :, h * C : (h + 1) * C]
    return total


def sum_blocks(slots, rows_ref, harm_rows_ref, zeroth_ref, table_ref, gates_ref, sums_ref, harm_sums_ref, first_ref):
    node = lax.broadcasted_iota(I32, (GN, GE), 0)
    edge = lax.broadcasted_iota(I32, (GN, GE), 1)
    same_block = lax.shift_right_logical(node, 1) == lax.shift_right_logical(edge, 5)
    wanted = jnp.where(same_block, lax.bitwise_and(node, 1), -1)

    def both(g, total):
        harmonic_sums(g, wanted, rows_ref, harm_rows_ref, zeroth_ref, harm_sums_ref, first_ref)
        for n in range(FIXED):
            total = sum_edges(g * FIXED + n, total, slots, table_ref, gates_ref, sums_ref)
        return total

    def rest(pair, total):
        for n in range(2):
            total = sum_edges(pair * 2 + n, total, slots, table_ref, gates_ref, sums_ref)
        return total

    total = lax.fori_loop(0, GROUPS, both, jnp.zeros((PARTS, 8, WIDE), F32))
    lax.fori_loop(GROUPS * FIXED // 2, slots[LISTS - 1][0], rest, total)


def update_nodes(nodes_ref, sums_ref, first_ref, harm_sums_ref, weight_ref, squares_ref, combined_ref):
    def one(lm, degree, left):
        left = jnp.concatenate([left, harm_sums_ref[lm]], axis=1).astype(BF16)
        mixed = jnp.dot(left, weight_ref[degree], preferred_element_type=F32)
        cut = pl.ds(pl.multiple_of(lm * C, C), C)
        value = nodes_ref[:, cut].astype(F32) + mixed
        combined_ref[:, cut] = value
        return value * value

    squares_ref[...] = one(0, 0, first_ref[...])

    @pl.loop(0, 48 // STEP)
    def _(step):
        squares = None
        for n in range(STEP):
            lm = step * STEP + n + 1
            degree = 1
            for d in range(2, DEG):
                degree = degree + (lm >= d * d).astype(I32)
            square = one(lm, degree, sums_ref[pl.ds(lm - 1, NODES, stride=ROWS), :])
            squares = square if squares is None else squares + square
        squares_ref[...] += squares


def store_nodes(squares_ref, gain_ref, combined_ref, out_ref, out_hbm, out_sem):
    mean = jnp.sum(squares_ref[...], axis=1, keepdims=True) / FEAT
    squares_ref[...] = jnp.broadcast_to(lax.rsqrt(mean + norm_eps), (NODES, C))

    def copy(n):
        cut = pl.ds(pl.multiple_of(n * BAND, BAND), BAND)
        return pltpu.make_async_copy(out_ref.at[cut], out_hbm.at[cut], out_sem.at[n])

    @pl.loop(0, NODES // BAND)
    def _(n):
        cut = pl.ds(pl.multiple_of(n * BAND, BAND), BAND)
        inverse = squares_ref[cut, :]
        for lm in range(0, COEF, 2):
            pair = []
            for at in range(lm, min(lm + 2, COEF)):
                degree = int(DEGREE_OF[at])
                pair.append(
                    combined_ref[cut, at * C : (at + 1) * C] * inverse * gain_ref[degree : degree + 1, :]
                )
            value = jnp.concatenate(pair, axis=1) if len(pair) == 2 else pair[0]
            out_ref[cut, lm * C : (lm + len(pair)) * C] = value.astype(BF16)
        copy(n).start()

    for n in range(NODES // BAND):
        copy(n).wait()


def layer_kernel(
    table_ref,
    gates_ref,
    rows_ref,
    harm_rows_ref,
    zeroth_ref,
    slot_ref,
    weight_ref,
    gain_ref,
    nodes_ref,
    out_hbm,
    sums_ref,
    harm_sums_ref,
    first_ref,
    squares_ref,
    combined_ref,
    out_ref,
    slot_sem,
    out_sem,
    *slots,
):
    slot_copies = []
    for n, slot in enumerate(slots):
        copy = pltpu.make_async_copy(slot_ref.at[n], slot, slot_sem.at[n])
        copy.start()
        slot_copies.append(copy)
    for copy in slot_copies:
        copy.wait()
    sum_blocks(
        slots, rows_ref, harm_rows_ref, zeroth_ref, table_ref, gates_ref, sums_ref, harm_sums_ref, first_ref
    )
    update_nodes(nodes_ref, sums_ref, first_ref, harm_sums_ref, weight_ref, squares_ref, combined_ref)
    store_nodes(squares_ref, gain_ref, combined_ref, out_ref, out_hbm, out_sem)


VMEM = pl.BlockSpec(memory_space=pltpu.VMEM)
ANY = pl.BlockSpec(memory_space=pl.ANY)
HBM = pl.BlockSpec(memory_space=pltpu.HBM)


def gather(*arrays, peers, columns):
    return pl.pallas_call(
        functools.partial(gather_kernel, peers=peers, columns=columns),
        out_shape=(
            pltpu.VMEM(((TABLE + 1) * PARTS, 8, WIDE), BF16),
            pltpu.VMEM((LENGTHS * PARTS, 8, WIDE), BF16),
            pltpu.VMEM((3, GROUPS, GE), I32),
            pltpu.VMEM((COEF * GROUPS, GE), F32),
            pltpu.VMEM((2, C, TABLE), BF16),
            pltpu.VMEM((40, LANES), I32),
            pltpu.VMEM((DEG, 2 * C, C), BF16),
        ),
        in_specs=[HBM] * 12,
        out_specs=(VMEM,) * 7,
        scratch_shapes=[
            pltpu.VMEM((4, HALO), I32),
            pltpu.VMEM((1, BLOCKS - KEEP), I32),
            pltpu.VMEM((EB, BLOCKS), I32),
            pltpu.VMEM((EB, BLOCKS), I32),
            pltpu.VMEM((EB, BLOCKS), BF16),
            pltpu.VMEM((HID, RB), BF16),
            pltpu.VMEM((COEF, EB, BLOCKS), BF16),
            pltpu.VMEM((DEG, C, C), BF16),
            pltpu.VMEM((C, C), BF16),
            pltpu.VMEM((DEG, C, C), BF16),
            pltpu.VMEM((NODES, FEAT), BF16),
            pltpu.VMEM((HID, DEG * C), BF16),
            pltpu.VMEM((4 * HALO, FEAT), BF16),
            pltpu.VMEM((4 * HALO, FEAT), BF16),
            pltpu.VMEM((LENGTHS, DEG * C), F32),
            pltpu.VMEM((LENGTHS, C), BF16),
            pltpu.VMEM((16 * ROWS, C), F32),
            pltpu.VMEM((TABLE, C), BF16),
            pltpu.VMEM((BLOCKS, EB), I32),
            pltpu.VMEM((BLOCKS, EB), I32),
            pltpu.VMEM((BLOCKS, EB), I32),
            pltpu.VMEM((7, BLOCKS, EB), F32),
            pltpu.VMEM((6, EB, BLOCKS), I32),
            pltpu.VMEM((4 * WORK, LANES), F32),
            pltpu.SemaphoreType.DMA((PIECES,)),
            pltpu.SemaphoreType.DMA((11,)),
            pltpu.SemaphoreType.DMA((4, PIECES)),
            pltpu.SemaphoreType.DMA((4, PIECES)),
        ],
        compiler_params=pltpu.CompilerParams(
            collective_id=0, has_side_effects=True, vmem_limit_bytes=GATHER_VMEM
        ),
        name="gather",
    )(*[pltpu.with_memory_space_constraint(a, pltpu.HBM) for a in arrays])


def layer(*arrays):
    return pl.pallas_call(
        layer_kernel,
        out_shape=jax.ShapeDtypeStruct((NODES, FEAT), BF16),
        in_specs=[VMEM] * len(arrays),
        out_specs=ANY,
        scratch_shapes=[
            pltpu.VMEM(((NODES + 1) * ROWS, C), F32),
            pltpu.VMEM((COEF, NODES, C), F32),
            pltpu.VMEM((NODES, C), F32),
            pltpu.VMEM((NODES, C), F32),
            pltpu.VMEM((NODES, FEAT), F32),
            pltpu.VMEM((NODES, FEAT), BF16),
            pltpu.SemaphoreType.DMA((LISTS,)),
            pltpu.SemaphoreType.DMA((NODES // BAND,)),
        ]
        + [pltpu.SMEM((LANES,), I32)] * LISTS,
        compiler_params=pltpu.CompilerParams(vmem_limit_bytes=LAYER_VMEM),
        name="layer",
    )(*arrays)


GATHER_VMEM = 22 * 1024 * 1024
LAYER_VMEM = 30 * 1024 * 1024


def per_device(
    node_feats,
    halo_index,
    edge_source,
    edge_target,
    edge_length,
    edge_harmonics,
    block_peer,
    radial_in,
    radial_out,
    mix_weight,
    harmonic_weight,
    update_weight,
    norm_gain,
):
    gathered = gather(
        node_feats,
        halo_index[0],
        block_peer,
        edge_source.T,
        edge_target.T,
        edge_length.T,
        radial_in.T,
        radial_out,
        edge_harmonics.transpose(2, 1, 0),
        mix_weight,
        harmonic_weight,
        update_weight,
        peers=lax.axis_size("gx"),
        columns=lax.axis_size("gy"),
    )
    return layer(*gathered, norm_gain, node_feats)


def solution(mesh):
    split = ("gx", "gy")
    in_specs = (
        P(split, None),
        P(split, None, None),
        P(split, None),
        P(split, None),
        P(split, None),
        P(split, None, None),
        P(split, None),
        P(),
        P(),
        P(),
        P(),
        P(),
        P(),
    )
    return jax.shard_map(
        per_device, mesh=mesh, in_specs=in_specs, out_specs=P(split, None), check_vma=False
    )
```

```python
import functools

import jax
import jax.numpy as jnp
import numpy as np
from jax import lax
from jax.experimental import pallas as pl
from jax.experimental.pallas import tpu as pltpu
from jax.sharding import PartitionSpec as P

LMAX = 6
DEG = 7
COEF = 49
C = 128
HID = 600
RB = 128
FEAT = 6272
EB = 32
TB = 2
KEEP = 96
BLOCKS = 128
NODES = 256
HALO = 32
TABLE = NODES + 4 * HALO
GROUP = 8
GROUPS = BLOCKS // GROUP
GE = GROUP * EB
GN = GROUP * TB
LENGTHS = 384
ROWS = 49
CHUNK = 4
CHUNKS = BLOCKS * (EB // CHUNK + 1)
WORK = 16
QUARTERS = WORK // CHUNK
STEPS = CHUNKS // QUARTERS
LANES = 384
LISTS = 2 * WORK + QUARTERS + 1
FIXED = 12

cutoff_radius = 6.0
norm_eps = 1e-06

F32 = jnp.float32
BF16 = jnp.bfloat16
I32 = jnp.int32

DEGREE_OF = np.repeat(np.arange(LMAX + 1), 2 * np.arange(LMAX + 1) + 1)
PARTS = 3
WIDE = 2 * C
STEP = 16
BAND = 32
PIECE = 7 * C
PIECES = FEAT // PIECE
MESH = pl.DeviceIdType.MESH


def length_index(length):
    r = length.astype(F32)
    f = jnp.where(
        r < 1.0,
        (r - 0.796875) * 256.0,
        jnp.where(
            r < 2.0,
            (r - 1.0) * 128.0 + 52.0,
            jnp.where(r < 4.0, (r - 2.0) * 64.0 + 180.0, (r - 4.0) * 32.0 + 308.0),
        ),
    )
    return f.astype(I32)


def length_of(i):
    return jnp.where(
        i < 52.0,
        0.796875 + i / 256.0,
        jnp.where(
            i < 180.0,
            1.0 + (i - 52.0) / 128.0,
            jnp.where(i < 308.0, 2.0 + (i - 180.0) / 64.0, 4.0 + (i - 308.0) / 32.0),
        ),
    )


def fill_basis(basis_ref):
    i = lax.broadcasted_iota(I32, (LENGTHS, RB), 0).astype(F32)
    r = length_of(i)
    k = lax.broadcasted_iota(I32, (LENGTHS, RB), 1).astype(F32)
    centers = cutoff_radius * (k + 0.5) / RB
    spread = 2.0 * cutoff_radius / RB
    along = length_of(lax.broadcasted_iota(I32, (8, LENGTHS), 1).astype(F32))
    envelope = (0.5 * (jnp.cos(jnp.pi * along / cutoff_radius) + 1.0)).T[:, :1]
    offsets = (r - centers) / spread
    basis_ref[...] = (jnp.exp(-0.5 * offsets * offsets) * envelope).astype(BF16)


def fill_gates(basis_ref, radial_in_ref, radial_out_ref, gate_ref, gate0_ref, table_ref):
    hidden = lax.dot_general(
        basis_ref[...], radial_in_ref[...], (((1,), (1,)), ((), ())), preferred_element_type=F32
    )
    half = 0.5 * hidden
    hidden = (half * jnp.tanh(half) + half).astype(BF16)
    gate = jnp.dot(hidden, radial_out_ref[...], preferred_element_type=F32).astype(BF16)
    gate0_ref[...] = gate[:, :C]
    gate_ref[...] = gate.astype(F32)
    row = lax.broadcasted_iota(I32, (8, C), 0)

    @pl.loop(0, LENGTHS // 8)
    def _(g):
        rows = [gate_ref[pl.ds(g * 8, 8), d * C : (d + 1) * C] for d in range(DEG)]
        at = g * (8 * PARTS)
        for j in range(8):
            tiles = []
            for tile in range(6):
                first = int(DEGREE_OF[1 + 8 * tile])
                last = int(DEGREE_OF[8 + 8 * tile])
                value = jnp.broadcast_to(rows[first][j : j + 1], (8, C))
                if last != first:
                    split = last * last - (1 + 8 * tile)
                    value = jnp.where(
                        row < split, value, jnp.broadcast_to(rows[last][j : j + 1], (8, C))
                    )
                tiles.append(value)
            for i in range(3):
                table_ref[at + j * PARTS + i] = jnp.concatenate(
                    tiles[2 * i : 2 * i + 2], axis=1
                ).astype(BF16)


def spread_rows(source_ref, count, first, base, wide_ref, table_ref):
    @pl.loop(0, count // 16)
    def _(g):
        at = pl.multiple_of(g * 16, 16)
        for lm in range(1, COEF, 2):
            pair = source_ref[pl.ds(pl.multiple_of(first + at, 16), 16), lm * C : (lm + 2) * C].astype(F32)
            wide_ref[pl.ds(lm - 1, 16, stride=ROWS), :] = pair[:, :C]
            wide_ref[pl.ds(lm, 16, stride=ROWS), :] = pair[:, C:]
        to = (base + at) * PARTS
        for j in range(16):
            for i in range(3):
                low = j * ROWS + 16 * i
                table_ref[to + j * PARTS + i] = jnp.concatenate(
                    [wide_ref[low : low + 8, :], wide_ref[low + 8 : low + 16, :]], axis=1
                ).astype(BF16)


def column_of(row, size):
    diagonal = lax.broadcasted_iota(I32, (size, size), 0) == lax.broadcasted_iota(I32, (size, size), 1)
    return jnp.sum(jnp.where(diagonal, jnp.broadcast_to(row, (size, size)), 0), axis=1, keepdims=True)


def fill_lists(
    peer_ref, source_ref, target_ref, length_ref, peers, across_refs, place_ref, list_ref, slot_ref
):
    peer = jnp.concatenate([jnp.zeros((1, KEEP), I32), peer_ref[...]], axis=1)
    target = jnp.where(peer < peers, target_ref[...], TB)
    source = source_ref[...]
    length = length_index(length_ref[...])
    for ref, value in zip(across_refs, (source, length, target)):
        ref[...] = value.T
    lower = (
        lax.broadcasted_iota(I32, (EB, EB), 0) > lax.broadcasted_iota(I32, (EB, EB), 1)
    ).astype(F32)
    zero = (target == 0).astype(F32)
    one = (target == 1).astype(F32)
    rank0 = jnp.dot(lower, zero, preferred_element_type=F32).astype(I32)
    rank1 = jnp.dot(lower, one, preferred_element_type=F32).astype(I32)

    def chunks(mask):
        count = jnp.sum(mask, axis=0, keepdims=True).astype(I32)
        return jnp.maximum(lax.shift_right_logical(count + (CHUNK - 1), 2), 1)

    chunks0, chunks1 = chunks(zero), chunks(one)
    before = (
        lax.broadcasted_iota(I32, (BLOCKS, BLOCKS), 0) < lax.broadcasted_iota(I32, (BLOCKS, BLOCKS), 1)
    ).astype(F32)
    each = jnp.broadcast_to((chunks0 + chunks1).astype(F32), (8, BLOCKS))
    start = jnp.dot(each, before, preferred_element_type=F32).astype(I32)
    start0 = start[:1]
    start1 = start0 + chunks0
    place = jnp.where(target == 0, start0 * CHUNK + rank0, start1 * CHUNK + rank1)
    place = jnp.where(target < TB, place, -1)
    source = source + 1
    for n, value in enumerate(
        (
            lax.bitwise_and(place, WORK - 1),
            lax.shift_right_arithmetic(place, 4),
            lax.shift_right_logical(source, 8),
            lax.bitwise_and(source, 255),
            lax.shift_right_logical(length, 8),
            lax.bitwise_and(length, 255),
        )
    ):
        place_ref[n] = value
    list_ref[...] = jnp.zeros((4 * WORK, LANES), F32)

    @pl.loop(0, EB // 4)
    def _(step):
        column = lax.broadcasted_iota(I32, (LANES, BLOCKS), 0)
        lane = lax.broadcasted_iota(I32, (WORK, BLOCKS), 0)
        total = None
        for half in range(2):
            lefts, rights = [], []
            for n in range(2):
                e = step * 4 + half * 2 + n
                row = [place_ref[m, pl.ds(e, 1), :] for m in range(6)]
                mine = lane == row[0]
                lefts.append(
                    jnp.concatenate([jnp.where(mine, row[m], 0) for m in range(2, 6)], axis=0)
                    .astype(F32)
                    .astype(BF16)
                )
                rights.append((column == row[1]).astype(F32).astype(BF16))
            product = lax.dot_general(
                jnp.concatenate(lefts, axis=1),
                jnp.concatenate(rights, axis=1),
                (((1,), (1,)), ((), ())),
                preferred_element_type=F32,
            )
            total = product if total is None else total + product
        list_ref[...] += total

    found = list_ref[...].astype(I32)
    slot_ref[:WORK, :] = (found[:WORK] * 256 + found[WORK : 2 * WORK]) * PARTS
    slot_ref[WORK : 2 * WORK, :] = (found[2 * WORK : 3 * WORK] * 256 + found[3 * WORK :]) * PARTS
    starts = jnp.concatenate([start0, start1, jnp.zeros((6, BLOCKS), I32)], axis=0).T
    count = (start1 + chunks1)[:, BLOCKS - 1 :]
    for q in range(QUARTERS):
        chunk = lax.broadcasted_iota(I32, (BLOCKS, LANES), 1) * QUARTERS + q
        reached = jnp.zeros((1, LANES), I32)
        opened = jnp.zeros((1, LANES), I32)
        for t in range(TB):
            column = starts[:, t : t + 1]
            reached = reached + jnp.sum((column <= chunk).astype(I32), axis=0, keepdims=True)
            opened = opened + jnp.sum((column == chunk).astype(I32), axis=0, keepdims=True)
        node = jnp.where(chunk[:1] < count, reached - 1, NODES)
        slot_ref[2 * WORK + q : 2 * WORK + q + 1, :] = node * (2 * ROWS) + opened
    slot_ref[LISTS - 1 : LISTS, :] = jnp.broadcast_to(
        lax.shift_right_logical(count + (2 * QUARTERS - 1), 3), (1, LANES)
    )


def by_group(ref):
    return jnp.concatenate([ref[pl.ds(b, GROUPS, stride=GROUP), :] for b in range(GROUP)], axis=1)


def transposed(x):
    rows = x.shape[1]
    identity = (
        lax.broadcasted_iota(I32, (rows, rows), 0) == lax.broadcasted_iota(I32, (rows, rows), 1)
    ).astype(F32).astype(BF16)
    return lax.dot_general(identity, x, (((1,), (1,)), ((), ())), preferred_element_type=F32)


def turn_harmonics(across_refs, harm_ref, turned_ref, rows_ref, harm_rows_ref):
    for n, ref in enumerate(across_refs):
        rows_ref[n] = by_group(ref)

    @pl.loop(0, COEF // 7)
    def _(step):
        for n in range(7):
            turned_ref[n] = harm_ref[step * 7 + n].astype(F32).T
            harm_rows_ref[step * 7 + n] = by_group(turned_ref.at[n])


def harmonic_sums(g, wanted, rows_ref, harm_rows_ref, zeroth_ref, harm_sums_ref, first_ref):
    across = (((1,), (1,)), ((), ()))
    row = lax.broadcasted_iota(I32, (TABLE, GE), 0)
    pick = (rows_ref[0, pl.ds(g, 1), :] == row).astype(F32).astype(BF16)
    scalar = jnp.dot(zeroth_ref[0], pick, preferred_element_type=F32).astype(BF16)
    pick = (rows_ref[1, pl.ds(g, 1), :] == row).astype(F32).astype(BF16)
    gate = jnp.dot(zeroth_ref[1], pick, preferred_element_type=F32).astype(BF16)
    mask = (rows_ref[2, pl.ds(g, 1), :] == wanted).astype(F32)
    at = pl.multiple_of(g * GN, GN)
    first_ref[pl.ds(at, GN), :] = lax.dot_general(
        mask.astype(BF16), scalar * gate, across, preferred_element_type=F32
    )
    left = jnp.concatenate(
        [(harm_rows_ref[lm, pl.ds(g, 1), :] * mask).astype(BF16) for lm in range(COEF)],
        axis=0,
    )
    right = lax.dot_general(left, scalar, across, preferred_element_type=F32)
    for lm in range(COEF):
        harm_sums_ref[lm, pl.ds(at, GN), :] = right[lm * GN : (lm + 1) * GN]


def gather_kernel(
    nodes_hbm,
    halo_hbm,
    peer_hbm,
    source_hbm,
    target_hbm,
    length_hbm,
    radial_in_hbm,
    radial_out_hbm,
    harm_hbm,
    mix_hbm,
    harmonic_hbm,
    update_hbm,
    table_ref,
    gates_ref,
    rows_ref,
    harm_rows_ref,
    gate_turned_ref,
    scalars_ref,
    slot_ref,
    weight_ref,
    halo_ref,
    peer_ref,
    source_ref,
    target_ref,
    length_ref,
    radial_in_ref,
    harm_ref,
    mix_ref,
    harmonic_ref,
    update_ref,
    nodes_ref,
    radial_out_ref,
    send_ref,
    arrived_ref,
    gate_ref,
    gate0_ref,
    wide_ref,
    source_across_ref,
    length_across_ref,
    target_across_ref,
    turned_ref,
    place_ref,
    list_ref,
    basis_ref,
    load_sem,
    other_sem,
    send_sem,
    recv_sem,
    peers,
    columns,
):
    p, q = lax.axis_index("gx"), lax.axis_index("gy")
    ahead, behind = lax.rem(p + 1, peers), lax.rem(p + peers - 1, peers)
    above, below = lax.rem(q + 1, columns), lax.rem(q + columns - 1, columns)
    neighbours = ((ahead, q), (behind, q), (p, above), (p, below))

    smalls = []
    for n, (source, target) in enumerate(
        (
            (halo_hbm, halo_ref),
            (peer_hbm, peer_ref),
            (source_hbm, source_ref),
            (target_hbm, target_ref),
            (length_hbm, length_ref),
            (radial_in_hbm, radial_in_ref),
            (radial_out_hbm, radial_out_ref),
            (harm_hbm, harm_ref),
            (mix_hbm, mix_ref),
            (harmonic_hbm, harmonic_ref),
            (update_hbm, update_ref),
        )
    ):
        smalls.append(pltpu.make_async_copy(source, target, other_sem.at[n]))
    smalls[0].start()
    loads = []
    for c in range(PIECES):
        cut = pl.ds(c * PIECE, PIECE)
        load = pltpu.make_async_copy(nodes_hbm.at[:, cut], nodes_ref.at[:, cut], load_sem.at[c])
        load.start()
        loads.append(load)
    for load in smalls[1:]:
        load.start()

    barrier = pltpu.get_barrier_semaphore()
    for neighbour in neighbours:
        pl.semaphore_signal(barrier, inc=1, device_id=neighbour, device_id_type=MESH)

    fill_basis(basis_ref)
    smalls[0].wait()
    index = column_of(jnp.concatenate([halo_ref[k : k + 1, :] for k in range(4)], axis=1), 4 * HALO)
    pick = (lax.broadcasted_iota(I32, (4 * HALO, NODES), 1) == index).astype(F32).astype(BF16)
    pl.semaphore_wait(barrier, 4)
    copies = []
    for c in range(PIECES):
        loads[c].wait()
        cut = pl.ds(c * PIECE, PIECE)
        send_ref[:, cut] = jnp.dot(pick, nodes_ref[:, cut], preferred_element_type=F32).astype(BF16)
        for k in (2, 3, 0, 1):
            part = pl.ds(k * HALO, HALO)
            copy = pltpu.make_async_remote_copy(
                src_ref=send_ref.at[part, cut],
                dst_ref=arrived_ref.at[part, cut],
                send_sem=send_sem.at[k, c],
                recv_sem=recv_sem.at[k, c],
                device_id=neighbours[k],
                device_id_type=MESH,
            )
            copy.start()
            copies.append(copy)

    for load in smalls[1:5]:
        load.wait()
    across_refs = (source_across_ref, length_across_ref, target_across_ref)
    fill_lists(
        peer_ref,
        source_ref,
        target_ref,
        length_ref,
        peers,
        across_refs,
        place_ref,
        list_ref,
        slot_ref,
    )
    smalls[5].wait()
    smalls[6].wait()
    fill_gates(basis_ref, radial_in_ref, radial_out_ref, gate_ref, gate0_ref, gates_ref)
    spread_rows(nodes_ref, NODES, 0, 1, wide_ref, table_ref)
    table_ref[:PARTS] = jnp.zeros((PARTS, 8, WIDE), BF16)
    smalls[7].wait()
    turn_harmonics(
        across_refs, harm_ref, turned_ref, rows_ref, harm_rows_ref
    )
    gate_turned_ref[...] = transposed(gate0_ref[...]).astype(BF16)
    for load in smalls[8:]:
        load.wait()
    for degree in range(DEG):
        both = jnp.concatenate([mix_ref[degree], harmonic_ref[...]], axis=0)
        weight_ref[degree] = jnp.dot(both, update_ref[degree], preferred_element_type=F32).astype(BF16)
    scalars_ref[:NODES, :] = nodes_ref[:, :C]
    for n, first in enumerate((2, 0)):
        for c in range(PIECES):
            for copy in copies[4 * c + first : 4 * c + first + 2]:
                copy.wait_recv()
        spread_rows(arrived_ref, 2 * HALO, 2 * HALO * n, NODES + 1 + 2 * HALO * n, wide_ref, table_ref)
    scalars_ref[NODES:, :] = arrived_ref[:, :C]
    for copy in copies:
        copy.wait_send()


def sum_edges(step, total, slots, table_ref, gates_ref, sums_ref):
    for q in range(QUARTERS):
        parts = []
        for k in range(q * CHUNK, (q + 1) * CHUNK):
            parts.append(
                table_ref[pl.ds(slots[k][step], PARTS)] * gates_ref[pl.ds(slots[WORK + k][step], PARTS)]
            )
        part = ((parts[0] + parts[1]) + (parts[2] + parts[3])).astype(F32)
        word = slots[2 * WORK + q][step]
        opens = lax.bitwise_and(jnp.full((1, 8, WIDE), word, I32), 1) == 1
        total = jnp.where(opens, part, total + part)
        at = lax.shift_right_logical(word, 1)
        for tile in range(6):
            i, h = divmod(tile, 2)
            sums_ref[pl.ds(at + 8 * tile, 8), :] = total[i, :, h * C : (h + 1) * C]
    return total


def sum_blocks(slots, rows_ref, harm_rows_ref, zeroth_ref, table_ref, gates_ref, sums_ref, harm_sums_ref, first_ref):
    node = lax.broadcasted_iota(I32, (GN, GE), 0)
    edge = lax.broadcasted_iota(I32, (GN, GE), 1)
    same_block = lax.shift_right_logical(node, 1) == lax.shift_right_logical(edge, 5)
    wanted = jnp.where(same_block, lax.bitwise_and(node, 1), -1)

    def both(g, total):
        for n in range(2):
            harmonic_sums(2 * g + n, wanted, rows_ref, harm_rows_ref, zeroth_ref, harm_sums_ref, first_ref)
        for n in range(2 * FIXED):
            total = sum_edges(g * 2 * FIXED + n, total, slots, table_ref, gates_ref, sums_ref)
        return total

    def rest(pair, total):
        for n in range(2):
            total = sum_edges(pair * 2 + n, total, slots, table_ref, gates_ref, sums_ref)
        return total

    total = lax.fori_loop(0, GROUPS // 2, both, jnp.zeros((PARTS, 8, WIDE), F32))
    lax.fori_loop(GROUPS * FIXED // 2, slots[LISTS - 1][0], rest, total)


def update_nodes(nodes_ref, sums_ref, first_ref, harm_sums_ref, weight_ref, squares_ref, combined_ref):
    def one(lm, degree, left):
        left = jnp.concatenate([left, harm_sums_ref[lm]], axis=1).astype(BF16)
        mixed = jnp.dot(left, weight_ref[degree], preferred_element_type=F32)
        cut = pl.ds(pl.multiple_of(lm * C, C), C)
        value = nodes_ref[:, cut].astype(F32) + mixed
        combined_ref[:, cut] = value
        return value * value

    squares_ref[...] = one(0, 0, first_ref[...])

    @pl.loop(0, 48 // STEP)
    def _(step):
        squares = None
        for n in range(STEP):
            lm = step * STEP + n + 1
            degree = 1
            for d in range(2, DEG):
                degree = degree + (lm >= d * d).astype(I32)
            square = one(lm, degree, sums_ref[pl.ds(lm - 1, NODES, stride=ROWS), :])
            squares = square if squares is None else squares + square
        squares_ref[...] += squares


def store_nodes(squares_ref, gain_ref, combined_ref, out_ref, out_hbm, out_sem):
    mean = jnp.sum(squares_ref[...], axis=1, keepdims=True) / FEAT
    squares_ref[...] = jnp.broadcast_to(lax.rsqrt(mean + norm_eps), (NODES, C))

    def copy(n):
        cut = pl.ds(pl.multiple_of(n * BAND, BAND), BAND)
        return pltpu.make_async_copy(out_ref.at[cut], out_hbm.at[cut], out_sem.at[n])

    @pl.loop(0, NODES // BAND)
    def _(n):
        cut = pl.ds(pl.multiple_of(n * BAND, BAND), BAND)
        inverse = squares_ref[cut, :]
        for lm in range(0, COEF, 2):
            pair = []
            for at in range(lm, min(lm + 2, COEF)):
                degree = int(DEGREE_OF[at])
                pair.append(
                    combined_ref[cut, at * C : (at + 1) * C] * inverse * gain_ref[degree : degree + 1, :]
                )
            value = jnp.concatenate(pair, axis=1) if len(pair) == 2 else pair[0]
            out_ref[cut, lm * C : (lm + len(pair)) * C] = value.astype(BF16)
        copy(n).start()

    for n in range(NODES // BAND):
        copy(n).wait()


def layer_kernel(
    table_ref,
    gates_ref,
    rows_ref,
    harm_rows_ref,
    gate_turned_ref,
    scalars_ref,
    slot_ref,
    weight_ref,
    gain_ref,
    nodes_ref,
    out_hbm,
    zeroth_ref,
    sums_ref,
    harm_sums_ref,
    first_ref,
    squares_ref,
    combined_ref,
    out_ref,
    slot_sem,
    out_sem,
    *slots,
):
    slot_copies = []
    for n, slot in enumerate(slots):
        copy = pltpu.make_async_copy(slot_ref.at[n], slot, slot_sem.at[n])
        copy.start()
        slot_copies.append(copy)
    zeroth_ref[0] = transposed(scalars_ref[...]).astype(BF16)
    zeroth_ref[1] = gate_turned_ref[...]
    for copy in slot_copies:
        copy.wait()
    sum_blocks(
        slots, rows_ref, harm_rows_ref, zeroth_ref, table_ref, gates_ref, sums_ref, harm_sums_ref, first_ref
    )
    update_nodes(nodes_ref, sums_ref, first_ref, harm_sums_ref, weight_ref, squares_ref, combined_ref)
    store_nodes(squares_ref, gain_ref, combined_ref, out_ref, out_hbm, out_sem)


VMEM = pl.BlockSpec(memory_space=pltpu.VMEM)
ANY = pl.BlockSpec(memory_space=pl.ANY)
HBM = pl.BlockSpec(memory_space=pltpu.HBM)


def gather(*arrays, peers, columns):
    return pl.pallas_call(
        functools.partial(gather_kernel, peers=peers, columns=columns),
        out_shape=(
            pltpu.VMEM(((TABLE + 1) * PARTS, 8, WIDE), BF16),
            pltpu.VMEM((LENGTHS * PARTS, 8, WIDE), BF16),
            pltpu.VMEM((3, GROUPS, GE), I32),
            pltpu.VMEM((COEF, GROUPS, GE), F32),
            pltpu.VMEM((C, LENGTHS), BF16),
            pltpu.VMEM((TABLE, C), BF16),
            pltpu.VMEM((40, LANES), I32),
            pltpu.VMEM((DEG, 2 * C, C), BF16),
        ),
        in_specs=[HBM] * 12,
        out_specs=(VMEM,) * 8,
        scratch_shapes=[
            pltpu.VMEM((4, HALO), I32),
            pltpu.VMEM((1, BLOCKS - KEEP), I32),
            pltpu.VMEM((EB, BLOCKS), I32),
            pltpu.VMEM((EB, BLOCKS), I32),
            pltpu.VMEM((EB, BLOCKS), BF16),
            pltpu.VMEM((HID, RB), BF16),
            pltpu.VMEM((COEF, EB, BLOCKS), BF16),
            pltpu.VMEM((DEG, C, C), BF16),
            pltpu.VMEM((C, C), BF16),
            pltpu.VMEM((DEG, C, C), BF16),
            pltpu.VMEM((NODES, FEAT), BF16),
            pltpu.VMEM((HID, DEG * C), BF16),
            pltpu.VMEM((4 * HALO, FEAT), BF16),
            pltpu.VMEM((4 * HALO, FEAT), BF16),
            pltpu.VMEM((LENGTHS, DEG * C), F32),
            pltpu.VMEM((LENGTHS, C), BF16),
            pltpu.VMEM((16 * ROWS, C), F32),
            pltpu.VMEM((BLOCKS, EB), I32),
            pltpu.VMEM((BLOCKS, EB), I32),
            pltpu.VMEM((BLOCKS, EB), I32),
            pltpu.VMEM((7, BLOCKS, EB), F32),
            pltpu.VMEM((6, EB, BLOCKS), I32),
            pltpu.VMEM((4 * WORK, LANES), F32),
            pltpu.VMEM((LENGTHS, RB), BF16),
            pltpu.SemaphoreType.DMA((PIECES,)),
            pltpu.SemaphoreType.DMA((11,)),
            pltpu.SemaphoreType.DMA((4, PIECES)),
            pltpu.SemaphoreType.DMA((4, PIECES)),
        ],
        compiler_params=pltpu.CompilerParams(
            collective_id=0, has_side_effects=True, vmem_limit_bytes=GATHER_VMEM
        ),
        name="gather",
    )(*[pltpu.with_memory_space_constraint(a, pltpu.HBM) for a in arrays])


def layer(*arrays):
    return pl.pallas_call(
        layer_kernel,
        out_shape=jax.ShapeDtypeStruct((NODES, FEAT), BF16),
        in_specs=[VMEM] * len(arrays),
        out_specs=ANY,
        scratch_shapes=[
            pltpu.VMEM((2, C, TABLE), BF16),
            pltpu.VMEM(((NODES + 1) * ROWS, C), F32),
            pltpu.VMEM((COEF, NODES, C), F32),
            pltpu.VMEM((NODES, C), F32),
            pltpu.VMEM((NODES, C), F32),
            pltpu.VMEM((NODES, FEAT), F32),
            pltpu.VMEM((NODES, FEAT), BF16),
            pltpu.SemaphoreType.DMA((LISTS,)),
            pltpu.SemaphoreType.DMA((NODES // BAND,)),
        ]
        + [pltpu.SMEM((LANES,), I32)] * LISTS,
        compiler_params=pltpu.CompilerParams(vmem_limit_bytes=LAYER_VMEM),
        name="layer",
    )(*arrays)


GATHER_VMEM = 22 * 1024 * 1024
LAYER_VMEM = 30 * 1024 * 1024


def per_device(
    node_feats,
    halo_index,
    edge_source,
    edge_target,
    edge_length,
    edge_harmonics,
    block_peer,
    radial_in,
    radial_out,
    mix_weight,
    harmonic_weight,
    update_weight,
    norm_gain,
):
    gathered = gather(
        node_feats,
        halo_index[0],
        block_peer,
        edge_source.T,
        edge_target.T,
        edge_length.T,
        radial_in.T,
        radial_out,
        edge_harmonics.transpose(2, 1, 0),
        mix_weight,
        harmonic_weight,
        update_weight,
        peers=lax.axis_size("gx"),
        columns=lax.axis_size("gy"),
    )
    return layer(*gathered, norm_gain, node_feats)


def solution(mesh):
    split = ("gx", "gy")
    in_specs = (
        P(split, None),
        P(split, None, None),
        P(split, None),
        P(split, None),
        P(split, None),
        P(split, None, None),
        P(split, None),
        P(),
        P(),
        P(),
        P(),
        P(),
        P(),
    )
    return jax.shard_map(
        per_device, mesh=mesh, in_specs=in_specs, out_specs=P(split, None), check_vma=False
    )
```

```python
import functools

import jax
import jax.numpy as jnp
import numpy as np
from jax import lax
from jax.experimental import pallas as pl
from jax.experimental.pallas import tpu as pltpu
from jax.sharding import PartitionSpec as P

LMAX = 6
DEG = 7
COEF = 49
C = 128
HID = 600
RB = 128
FEAT = 6272
EB = 32
TB = 2
KEEP = 96
BLOCKS = 128
NODES = 256
HALO = 32
TABLE = NODES + 4 * HALO
GROUP = 8
GROUPS = BLOCKS // GROUP
GE = GROUP * EB
GN = GROUP * TB
LENGTHS = 384
ROWS = 49
CHUNK = 4
CHUNKS = BLOCKS * (EB // CHUNK + 1)
WORK = 16
QUARTERS = WORK // CHUNK
STEPS = CHUNKS // QUARTERS
LANES = 384
LISTS = 2 * WORK + QUARTERS + 1
FIXED = 28

cutoff_radius = 6.0
norm_eps = 1e-06

F32 = jnp.float32
BF16 = jnp.bfloat16
I32 = jnp.int32

DEGREE_OF = np.repeat(np.arange(LMAX + 1), 2 * np.arange(LMAX + 1) + 1)
PARTS = 3
WIDE = 2 * C
STEP = 16
BAND = 32
SIZES = (2, 4, 6, 9, 9, 9, 10)
CUTS = tuple((C * sum(SIZES[:n]), C * size) for n, size in enumerate(SIZES))
PIECES = len(CUTS)
MESH = pl.DeviceIdType.MESH


def length_index(length):
    r = length.astype(F32)
    f = jnp.where(
        r < 1.0,
        (r - 0.796875) * 256.0,
        jnp.where(
            r < 2.0,
            (r - 1.0) * 128.0 + 52.0,
            jnp.where(r < 4.0, (r - 2.0) * 64.0 + 180.0, (r - 4.0) * 32.0 + 308.0),
        ),
    )
    return f.astype(I32)


def length_of(i):
    return jnp.where(
        i < 52.0,
        0.796875 + i / 256.0,
        jnp.where(
            i < 180.0,
            1.0 + (i - 52.0) / 128.0,
            jnp.where(i < 308.0, 2.0 + (i - 180.0) / 64.0, 4.0 + (i - 308.0) / 32.0),
        ),
    )


def fill_basis(basis_ref):
    i = lax.broadcasted_iota(I32, (LENGTHS, RB), 0).astype(F32)
    r = length_of(i)
    k = lax.broadcasted_iota(I32, (LENGTHS, RB), 1).astype(F32)
    centers = cutoff_radius * (k + 0.5) / RB
    spread = 2.0 * cutoff_radius / RB
    along = length_of(lax.broadcasted_iota(I32, (8, LENGTHS), 1).astype(F32))
    envelope = (0.5 * (jnp.cos(jnp.pi * along / cutoff_radius) + 1.0)).T[:, :1]
    offsets = (r - centers) / spread
    basis_ref[...] = (jnp.exp(-0.5 * offsets * offsets) * envelope).astype(BF16)


def fill_gates(basis_ref, radial_in_ref, radial_out_ref, gate_ref, gate0_ref, table_ref):
    hidden = lax.dot_general(
        basis_ref[...], radial_in_ref[...], (((1,), (1,)), ((), ())), preferred_element_type=F32
    )
    half = 0.5 * hidden
    hidden = (half * jnp.tanh(half) + half).astype(BF16)
    gate = jnp.dot(hidden, radial_out_ref[...], preferred_element_type=F32).astype(BF16)
    gate0_ref[...] = gate[:, :C]
    gate_ref[...] = gate.astype(F32)
    row = lax.broadcasted_iota(I32, (8, C), 0)

    @pl.loop(0, LENGTHS // 8)
    def _(g):
        rows = [gate_ref[pl.ds(g * 8, 8), d * C : (d + 1) * C] for d in range(DEG)]
        at = g * (8 * PARTS)
        for j in range(8):
            tiles = []
            for tile in range(6):
                first = int(DEGREE_OF[1 + 8 * tile])
                last = int(DEGREE_OF[8 + 8 * tile])
                value = jnp.broadcast_to(rows[first][j : j + 1], (8, C))
                if last != first:
                    split = last * last - (1 + 8 * tile)
                    value = jnp.where(
                        row < split, value, jnp.broadcast_to(rows[last][j : j + 1], (8, C))
                    )
                tiles.append(value)
            for i in range(3):
                table_ref[at + j * PARTS + i] = jnp.concatenate(
                    tiles[2 * i : 2 * i + 2], axis=1
                ).astype(BF16)


def spread_rows(source_ref, count, first, base, wide_ref, table_ref):
    @pl.loop(0, count // 16)
    def _(g):
        at = pl.multiple_of(g * 16, 16)
        for lm in range(1, COEF, 2):
            pair = source_ref[pl.ds(pl.multiple_of(first + at, 16), 16), lm * C : (lm + 2) * C].astype(F32)
            wide_ref[pl.ds(lm - 1, 16, stride=ROWS), :] = pair[:, :C]
            wide_ref[pl.ds(lm, 16, stride=ROWS), :] = pair[:, C:]
        to = (base + at) * PARTS
        for j in range(16):
            for i in range(3):
                low = j * ROWS + 16 * i
                table_ref[to + j * PARTS + i] = jnp.concatenate(
                    [wide_ref[low : low + 8, :], wide_ref[low + 8 : low + 16, :]], axis=1
                ).astype(BF16)


def column_of(row, size):
    diagonal = lax.broadcasted_iota(I32, (size, size), 0) == lax.broadcasted_iota(I32, (size, size), 1)
    return jnp.sum(jnp.where(diagonal, jnp.broadcast_to(row, (size, size)), 0), axis=1, keepdims=True)


def fill_lists(
    peer_ref, source_ref, target_ref, length_ref, peers, across_refs, place_ref, list_ref, slot_ref
):
    peer = jnp.concatenate([jnp.zeros((1, KEEP), I32), peer_ref[...]], axis=1)
    target = jnp.where(peer < peers, target_ref[...], TB)
    source = source_ref[...]
    length = length_index(length_ref[...])
    for ref, value in zip(across_refs, (source, length, target)):
        ref[...] = value.T
    lower = (
        lax.broadcasted_iota(I32, (EB, EB), 0) > lax.broadcasted_iota(I32, (EB, EB), 1)
    ).astype(F32)
    zero = (target == 0).astype(F32)
    one = (target == 1).astype(F32)
    rank0 = jnp.dot(lower, zero, preferred_element_type=F32).astype(I32)
    rank1 = jnp.dot(lower, one, preferred_element_type=F32).astype(I32)

    def chunks(mask):
        count = jnp.sum(mask, axis=0, keepdims=True).astype(I32)
        return jnp.maximum(lax.shift_right_logical(count + (CHUNK - 1), 2), 1)

    chunks0, chunks1 = chunks(zero), chunks(one)
    before = (
        lax.broadcasted_iota(I32, (BLOCKS, BLOCKS), 0) < lax.broadcasted_iota(I32, (BLOCKS, BLOCKS), 1)
    ).astype(F32)
    each = jnp.broadcast_to((chunks0 + chunks1).astype(F32), (8, BLOCKS))
    start = jnp.dot(each, before, preferred_element_type=F32).astype(I32)
    start0 = start[:1]
    start1 = start0 + chunks0
    place = jnp.where(target == 0, start0 * CHUNK + rank0, start1 * CHUNK + rank1)
    place = jnp.where(target < TB, place, -1)
    source = source + 1
    for n, value in enumerate(
        (
            lax.bitwise_and(place, WORK - 1),
            lax.shift_right_arithmetic(place, 4),
            lax.shift_right_logical(source, 8),
            lax.bitwise_and(source, 255),
            lax.shift_right_logical(length, 8),
            lax.bitwise_and(length, 255),
        )
    ):
        place_ref[n] = value
    list_ref[...] = jnp.zeros((4 * WORK, STEPS), F32)

    @pl.loop(0, EB // 4)
    def _(step):
        column = lax.broadcasted_iota(I32, (STEPS, BLOCKS), 0)
        lane = lax.broadcasted_iota(I32, (WORK, BLOCKS), 0)
        total = None
        for half in range(2):
            lefts, rights = [], []
            for n in range(2):
                e = step * 4 + half * 2 + n
                row = [place_ref[m, pl.ds(e, 1), :] for m in range(6)]
                mine = lane == row[0]
                lefts.append(
                    jnp.concatenate([jnp.where(mine, row[m], 0) for m in range(2, 6)], axis=0)
                    .astype(F32)
                    .astype(BF16)
                )
                rights.append((column == row[1]).astype(F32).astype(BF16))
            product = lax.dot_general(
                jnp.concatenate(lefts, axis=1),
                jnp.concatenate(rights, axis=1),
                (((1,), (1,)), ((), ())),
                preferred_element_type=F32,
            )
            total = product if total is None else total + product
        list_ref[...] += total

    found = jnp.concatenate(
        [list_ref[...].astype(I32), jnp.zeros((4 * WORK, LANES - STEPS), I32)], axis=1
    )
    slot_ref[:WORK, :] = (found[:WORK] * 256 + found[WORK : 2 * WORK]) * PARTS
    slot_ref[WORK : 2 * WORK, :] = (found[2 * WORK : 3 * WORK] * 256 + found[3 * WORK :]) * PARTS
    starts = jnp.concatenate([start0, start1, jnp.zeros((6, BLOCKS), I32)], axis=0).T
    count = (start1 + chunks1)[:, BLOCKS - 1 :]
    for q in range(QUARTERS):
        chunk = lax.broadcasted_iota(I32, (BLOCKS, LANES), 1) * QUARTERS + q
        reached = jnp.zeros((1, LANES), I32)
        opened = jnp.zeros((1, LANES), I32)
        for t in range(TB):
            column = starts[:, t : t + 1]
            reached = reached + jnp.sum((column <= chunk).astype(I32), axis=0, keepdims=True)
            opened = opened + jnp.sum((column == chunk).astype(I32), axis=0, keepdims=True)
        node = jnp.where(chunk[:1] < count, reached - 1, NODES)
        slot_ref[2 * WORK + q : 2 * WORK + q + 1, :] = node * (2 * ROWS) + opened
    slot_ref[LISTS - 1 : LISTS, :] = jnp.broadcast_to(
        lax.shift_right_logical(count + (2 * QUARTERS - 1), 3), (1, LANES)
    )


def by_group(ref):
    return jnp.concatenate([ref[pl.ds(b, GROUPS, stride=GROUP), :] for b in range(GROUP)], axis=1)


def transposed(x):
    rows = x.shape[1]
    identity = (
        lax.broadcasted_iota(I32, (rows, rows), 0) == lax.broadcasted_iota(I32, (rows, rows), 1)
    ).astype(F32).astype(BF16)
    return lax.dot_general(identity, x, (((1,), (1,)), ((), ())), preferred_element_type=F32)


def turn_harmonics(across_refs, harm_ref, turned_ref, rows_ref, harm_rows_ref):
    for n, ref in enumerate(across_refs):
        rows_ref[n] = by_group(ref)

    @pl.loop(0, COEF // 7)
    def _(step):
        for n in range(7):
            turned_ref[n] = harm_ref[step * 7 + n].astype(F32).T
            harm_rows_ref[step * 7 + n] = by_group(turned_ref.at[n])


def harmonic_sums(g, wanted, rows_ref, harm_rows_ref, zeroth_ref, harm_sums_ref, first_ref):
    across = (((1,), (1,)), ((), ()))
    row = lax.broadcasted_iota(I32, (TABLE, GE), 0)
    pick = (rows_ref[0, pl.ds(g, 1), :] == row).astype(F32).astype(BF16)
    scalar = jnp.dot(zeroth_ref[0], pick, preferred_element_type=F32).astype(BF16)
    pick = (rows_ref[1, pl.ds(g, 1), :] == row).astype(F32).astype(BF16)
    gate = jnp.dot(zeroth_ref[1], pick, preferred_element_type=F32).astype(BF16)
    mask = (rows_ref[2, pl.ds(g, 1), :] == wanted).astype(F32)
    at = pl.multiple_of(g * GN, GN)
    first_ref[pl.ds(at, GN), :] = lax.dot_general(
        mask.astype(BF16), scalar * gate, across, preferred_element_type=F32
    )
    left = jnp.concatenate(
        [(harm_rows_ref[lm, pl.ds(g, 1), :] * mask).astype(BF16) for lm in range(COEF)],
        axis=0,
    )
    right = lax.dot_general(left, scalar, across, preferred_element_type=F32)
    for lm in range(COEF):
        harm_sums_ref[lm, pl.ds(at, GN), :] = right[lm * GN : (lm + 1) * GN]


def gather_kernel(
    nodes_hbm,
    halo_hbm,
    peer_hbm,
    source_hbm,
    target_hbm,
    length_hbm,
    radial_in_hbm,
    radial_out_hbm,
    harm_hbm,
    mix_hbm,
    harmonic_hbm,
    update_hbm,
    table_ref,
    gates_ref,
    rows_ref,
    harm_rows_ref,
    gate_turned_ref,
    scalars_ref,
    slot_ref,
    weight_ref,
    halo_ref,
    peer_ref,
    source_ref,
    target_ref,
    length_ref,
    radial_in_ref,
    harm_ref,
    mix_ref,
    harmonic_ref,
    update_ref,
    nodes_ref,
    radial_out_ref,
    send_ref,
    arrived_ref,
    gate_ref,
    gate0_ref,
    wide_ref,
    source_across_ref,
    length_across_ref,
    target_across_ref,
    turned_ref,
    place_ref,
    list_ref,
    basis_ref,
    load_sem,
    other_sem,
    send_sem,
    recv_sem,
    peers,
    columns,
):
    p, q = lax.axis_index("gx"), lax.axis_index("gy")
    ahead, behind = lax.rem(p + 1, peers), lax.rem(p + peers - 1, peers)
    above, below = lax.rem(q + 1, columns), lax.rem(q + columns - 1, columns)
    neighbours = ((ahead, q), (behind, q), (p, above), (p, below))

    smalls = []
    for n, (source, target) in enumerate(
        (
            (halo_hbm, halo_ref),
            (peer_hbm, peer_ref),
            (source_hbm, source_ref),
            (target_hbm, target_ref),
            (length_hbm, length_ref),
            (radial_in_hbm, radial_in_ref),
            (radial_out_hbm, radial_out_ref),
            (harm_hbm, harm_ref),
            (mix_hbm, mix_ref),
            (harmonic_hbm, harmonic_ref),
            (update_hbm, update_ref),
        )
    ):
        smalls.append(pltpu.make_async_copy(source, target, other_sem.at[n]))
    smalls[0].start()
    loads = []
    for c in range(PIECES):
        cut = pl.ds(*CUTS[c])
        load = pltpu.make_async_copy(nodes_hbm.at[:, cut], nodes_ref.at[:, cut], load_sem.at[c])
        load.start()
        loads.append(load)
    for load in smalls[1:]:
        load.start()

    barrier = pltpu.get_barrier_semaphore()
    for neighbour in neighbours:
        pl.semaphore_signal(barrier, inc=1, device_id=neighbour, device_id_type=MESH)

    fill_basis(basis_ref)
    smalls[0].wait()
    index = column_of(jnp.concatenate([halo_ref[k : k + 1, :] for k in range(4)], axis=1), 4 * HALO)
    pick = (lax.broadcasted_iota(I32, (4 * HALO, NODES), 1) == index).astype(F32).astype(BF16)
    pl.semaphore_wait(barrier, 4)

    def send(k, c, cut):
        part = pl.ds(k * HALO, HALO)
        copy = pltpu.make_async_remote_copy(
            src_ref=send_ref.at[part, cut],
            dst_ref=arrived_ref.at[part, cut],
            send_sem=send_sem.at[k, c],
            recv_sem=recv_sem.at[k, c],
            device_id=neighbours[k],
            device_id_type=MESH,
        )
        copy.start()
        return copy

    above_below = []
    for c in range(PIECES):
        loads[c].wait()
        cut = pl.ds(*CUTS[c])
        send_ref[:, cut] = jnp.dot(pick, nodes_ref[:, cut], preferred_element_type=F32).astype(BF16)
        for k in (2, 3):
            above_below.append(send(k, c, cut))
    ahead_behind = [send(k, 0, pl.ds(0, FEAT)) for k in (0, 1)]

    for load in smalls[1:5]:
        load.wait()
    across_refs = (source_across_ref, length_across_ref, target_across_ref)
    fill_lists(
        peer_ref,
        source_ref,
        target_ref,
        length_ref,
        peers,
        across_refs,
        place_ref,
        list_ref,
        slot_ref,
    )
    smalls[5].wait()
    smalls[6].wait()
    fill_gates(basis_ref, radial_in_ref, radial_out_ref, gate_ref, gate0_ref, gates_ref)
    spread_rows(nodes_ref, NODES, 0, 1, wide_ref, table_ref)
    table_ref[:PARTS] = jnp.zeros((PARTS, 8, WIDE), BF16)
    smalls[7].wait()
    turn_harmonics(
        across_refs, harm_ref, turned_ref, rows_ref, harm_rows_ref
    )
    gate_turned_ref[...] = transposed(gate0_ref[...]).astype(BF16)
    for load in smalls[8:]:
        load.wait()
    for degree in range(DEG):
        both = jnp.concatenate([mix_ref[degree], harmonic_ref[...]], axis=0)
        weight_ref[degree] = jnp.dot(both, update_ref[degree], preferred_element_type=F32).astype(BF16)
    scalars_ref[:NODES, :] = nodes_ref[:, :C]
    for n, copies in enumerate((ahead_behind, above_below)):
        for copy in copies:
            copy.wait_recv()
        spread_rows(arrived_ref, 2 * HALO, 2 * HALO * n, NODES + 1 + 2 * HALO * n, wide_ref, table_ref)
    scalars_ref[NODES:, :] = arrived_ref[:, :C]
    for copy in ahead_behind + above_below:
        copy.wait_send()


def sum_edges(step, total, slots, table_ref, gates_ref, sums_ref):
    for q in range(QUARTERS):
        parts = []
        for k in range(q * CHUNK, (q + 1) * CHUNK):
            parts.append(
                table_ref[pl.ds(slots[k][step], PARTS)] * gates_ref[pl.ds(slots[WORK + k][step], PARTS)]
            )
        part = ((parts[0] + parts[1]) + (parts[2] + parts[3])).astype(F32)
        word = slots[2 * WORK + q][step]
        opens = lax.bitwise_and(jnp.full((1, 8, WIDE), word, I32), 1) == 1
        total = jnp.where(opens, part, total + part)
        at = lax.shift_right_logical(word, 1)
        for tile in range(6):
            i, h = divmod(tile, 2)
            sums_ref[pl.ds(at + 8 * tile, 8), :] = total[i, :, h * C : (h + 1) * C]
    return total


def sum_blocks(slot_copies, slots, rows_ref, harm_rows_ref, zeroth_ref, table_ref, gates_ref, sums_ref, harm_sums_ref, first_ref):
    node = lax.broadcasted_iota(I32, (GN, GE), 0)
    edge = lax.broadcasted_iota(I32, (GN, GE), 1)
    same_block = lax.shift_right_logical(node, 1) == lax.shift_right_logical(edge, 5)
    wanted = jnp.where(same_block, lax.bitwise_and(node, 1), -1)

    for n in range(2):
        harmonic_sums(n, wanted, rows_ref, harm_rows_ref, zeroth_ref, harm_sums_ref, first_ref)
    for copy in slot_copies:
        copy.wait()

    def both(g, total):
        for n in range(2):
            harmonic_sums(2 * g + 2 + n, wanted, rows_ref, harm_rows_ref, zeroth_ref, harm_sums_ref, first_ref)
        for n in range(FIXED):
            total = sum_edges(g * FIXED + n, total, slots, table_ref, gates_ref, sums_ref)
        return total

    def rest(pair, total):
        for n in range(2):
            total = sum_edges(pair * 2 + n, total, slots, table_ref, gates_ref, sums_ref)
        return total

    total = lax.fori_loop(0, GROUPS // 2 - 1, both, jnp.zeros((PARTS, 8, WIDE), F32))
    lax.fori_loop((GROUPS // 2 - 1) * FIXED // 2, slots[LISTS - 1][0], rest, total)


def update_nodes(nodes_ref, sums_ref, first_ref, harm_sums_ref, weight_ref, squares_ref, combined_ref):
    def one(lm, degree, left):
        left = jnp.concatenate([left, harm_sums_ref[lm]], axis=1).astype(BF16)
        mixed = jnp.dot(left, weight_ref[degree], preferred_element_type=F32)
        cut = pl.ds(pl.multiple_of(lm * C, C), C)
        value = nodes_ref[:, cut].astype(F32) + mixed
        combined_ref[:, cut] = value
        return value * value

    squares_ref[...] = one(0, 0, first_ref[...])

    @pl.loop(0, 48 // STEP)
    def _(step):
        squares = None
        for n in range(STEP):
            lm = step * STEP + n + 1
            degree = 1
            for d in range(2, DEG):
                degree = degree + (lm >= d * d).astype(I32)
            square = one(lm, degree, sums_ref[pl.ds(lm - 1, NODES, stride=ROWS), :])
            squares = square if squares is None else squares + square
        squares_ref[...] += squares


def store_nodes(squares_ref, gain_ref, combined_ref, out_ref, out_hbm, out_sem):
    mean = jnp.sum(squares_ref[...], axis=1, keepdims=True) / FEAT
    squares_ref[...] = jnp.broadcast_to(lax.rsqrt(mean + norm_eps), (NODES, C))

    def copy(n):
        cut = pl.ds(pl.multiple_of(n * BAND, BAND), BAND)
        return pltpu.make_async_copy(out_ref.at[cut], out_hbm.at[cut], out_sem.at[n])

    @pl.loop(0, NODES // BAND)
    def _(n):
        cut = pl.ds(pl.multiple_of(n * BAND, BAND), BAND)
        inverse = squares_ref[cut, :]
        for lm in range(0, COEF, 2):
            pair = []
            for at in range(lm, min(lm + 2, COEF)):
                degree = int(DEGREE_OF[at])
                pair.append(
                    combined_ref[cut, at * C : (at + 1) * C] * inverse * gain_ref[degree : degree + 1, :]
                )
            value = jnp.concatenate(pair, axis=1) if len(pair) == 2 else pair[0]
            out_ref[cut, lm * C : (lm + len(pair)) * C] = value.astype(BF16)
        copy(n).start()

    for n in range(NODES // BAND):
        copy(n).wait()


def layer_kernel(
    table_ref,
    gates_ref,
    rows_ref,
    harm_rows_ref,
    gate_turned_ref,
    scalars_ref,
    slot_ref,
    weight_ref,
    gain_ref,
    nodes_ref,
    out_hbm,
    zeroth_ref,
    sums_ref,
    harm_sums_ref,
    first_ref,
    squares_ref,
    combined_ref,
    out_ref,
    slot_sem,
    out_sem,
    *slots,
):
    slot_copies = []
    for n, slot in enumerate(slots):
        copy = pltpu.make_async_copy(slot_ref.at[n], slot, slot_sem.at[n])
        copy.start()
        slot_copies.append(copy)
    zeroth_ref[0] = transposed(scalars_ref[...]).astype(BF16)
    zeroth_ref[1] = gate_turned_ref[...]
    sum_blocks(
        slot_copies, slots, rows_ref, harm_rows_ref, zeroth_ref, table_ref, gates_ref, sums_ref, harm_sums_ref, first_ref
    )
    update_nodes(nodes_ref, sums_ref, first_ref, harm_sums_ref, weight_ref, squares_ref, combined_ref)
    store_nodes(squares_ref, gain_ref, combined_ref, out_ref, out_hbm, out_sem)


VMEM = pl.BlockSpec(memory_space=pltpu.VMEM)
ANY = pl.BlockSpec(memory_space=pl.ANY)
HBM = pl.BlockSpec(memory_space=pltpu.HBM)


def gather(*arrays, peers, columns):
    return pl.pallas_call(
        functools.partial(gather_kernel, peers=peers, columns=columns),
        out_shape=(
            pltpu.VMEM(((TABLE + 1) * PARTS, 8, WIDE), BF16),
            pltpu.VMEM((LENGTHS * PARTS, 8, WIDE), BF16),
            pltpu.VMEM((3, GROUPS, GE), I32),
            pltpu.VMEM((COEF, GROUPS, GE), F32),
            pltpu.VMEM((C, LENGTHS), BF16),
            pltpu.VMEM((TABLE, C), BF16),
            pltpu.VMEM((40, LANES), I32),
            pltpu.VMEM((DEG, 2 * C, C), BF16),
        ),
        in_specs=[HBM] * 12,
        out_specs=(VMEM,) * 8,
        scratch_shapes=[
            pltpu.VMEM((4, HALO), I32),
            pltpu.VMEM((1, BLOCKS - KEEP), I32),
            pltpu.VMEM((EB, BLOCKS), I32),
            pltpu.VMEM((EB, BLOCKS), I32),
            pltpu.VMEM((EB, BLOCKS), BF16),
            pltpu.VMEM((HID, RB), BF16),
            pltpu.VMEM((COEF, EB, BLOCKS), BF16),
            pltpu.VMEM((DEG, C, C), BF16),
            pltpu.VMEM((C, C), BF16),
            pltpu.VMEM((DEG, C, C), BF16),
            pltpu.VMEM((NODES, FEAT), BF16),
            pltpu.VMEM((HID, DEG * C), BF16),
            pltpu.VMEM((4 * HALO, FEAT), BF16),
            pltpu.VMEM((4 * HALO, FEAT), BF16),
            pltpu.VMEM((LENGTHS, DEG * C), F32),
            pltpu.VMEM((LENGTHS, C), BF16),
            pltpu.VMEM((16 * ROWS, C), F32),
            pltpu.VMEM((BLOCKS, EB), I32),
            pltpu.VMEM((BLOCKS, EB), I32),
            pltpu.VMEM((BLOCKS, EB), I32),
            pltpu.VMEM((7, BLOCKS, EB), F32),
            pltpu.VMEM((6, EB, BLOCKS), I32),
            pltpu.VMEM((4 * WORK, STEPS), F32),
            pltpu.VMEM((LENGTHS, RB), BF16),
            pltpu.SemaphoreType.DMA((PIECES,)),
            pltpu.SemaphoreType.DMA((11,)),
            pltpu.SemaphoreType.DMA((4, PIECES)),
            pltpu.SemaphoreType.DMA((4, PIECES)),
        ],
        compiler_params=pltpu.CompilerParams(
            collective_id=0, has_side_effects=True, vmem_limit_bytes=GATHER_VMEM
        ),
        name="gather",
    )(*[pltpu.with_memory_space_constraint(a, pltpu.HBM) for a in arrays])


def layer(*arrays):
    return pl.pallas_call(
        layer_kernel,
        out_shape=jax.ShapeDtypeStruct((NODES, FEAT), BF16),
        in_specs=[VMEM] * len(arrays),
        out_specs=ANY,
        scratch_shapes=[
            pltpu.VMEM((2, C, TABLE), BF16),
            pltpu.VMEM(((NODES + 1) * ROWS, C), F32),
            pltpu.VMEM((COEF, NODES, C), F32),
            pltpu.VMEM((NODES, C), F32),
            pltpu.VMEM((NODES, C), F32),
            pltpu.VMEM((NODES, FEAT), F32),
            pltpu.VMEM((NODES, FEAT), BF16),
            pltpu.SemaphoreType.DMA((LISTS,)),
            pltpu.SemaphoreType.DMA((NODES // BAND,)),
        ]
        + [pltpu.SMEM((LANES,), I32)] * LISTS,
        compiler_params=pltpu.CompilerParams(vmem_limit_bytes=LAYER_VMEM),
        name="layer",
    )(*arrays)


GATHER_VMEM = 22 * 1024 * 1024
LAYER_VMEM = 30 * 1024 * 1024


def per_device(
    node_feats,
    halo_index,
    edge_source,
    edge_target,
    edge_length,
    edge_harmonics,
    block_peer,
    radial_in,
    radial_out,
    mix_weight,
    harmonic_weight,
    update_weight,
    norm_gain,
):
    gathered = gather(
        node_feats,
        halo_index[0],
        block_peer,
        edge_source.T,
        edge_target.T,
        edge_length.T,
        radial_in.T,
        radial_out,
        edge_harmonics.transpose(2, 1, 0),
        mix_weight,
        harmonic_weight,
        update_weight,
        peers=lax.axis_size("gx"),
        columns=lax.axis_size("gy"),
    )
    return layer(*gathered, norm_gain, node_feats)


def solution(mesh):
    split = ("gx", "gy")
    in_specs = (
        P(split, None),
        P(split, None, None),
        P(split, None),
        P(split, None),
        P(split, None),
        P(split, None, None),
        P(split, None),
        P(),
        P(),
        P(),
        P(),
        P(),
        P(),
    )
    return jax.shard_map(
        per_device, mesh=mesh, in_specs=in_specs, out_specs=P(split, None), check_vma=False
    )
```
